256 devices in a mesh: grp: 2 (over z_lo), seq: 16 (over z_hi, y), tp: 8 (over x, core).
Axes of the slice: x: 4, y: 4, z: 8 (z_hi: 4, z_lo: 2; z = z_hi * 2 + z_lo), core: 2. Of those that a mesh axis runs over, the one named last changes fastest.
Arguments:
- teacher_in: bfloat16 [256, 8192], P(None, ('grp', 'tp')), may hold values from -6 to 6
- teacher_gain: float32 [8192], P(('grp', 'tp')), may hold values from 0.1 to 1.9
- teacher_gate: bfloat16 [2, 8192, 14336], P(None, ('grp', 'tp'), 'seq'), may hold values from -0.0625 to 0.0625
- teacher_up: bfloat16 [2, 8192, 14336], P(None, ('grp', 'tp'), 'seq'), may hold values from -0.0625 to 0.0625
- teacher_down: bfloat16 [2, 14336, 8192], P(None, 'seq', ('grp', 'tp')), may hold values from -0.046875 to 0.046875
- align_layer: int32 [256], replicated, may hold values from 0 to 1
- student_in: bfloat16 [256, 4096], P(None, 'seq'), may hold values from -6 to 6
- student_gain: float32 [4096], P('seq'), may hold values from 0.1 to 1.9
- student_gate: bfloat16 [4096, 14336], P('seq', ('grp', 'tp')), may hold values from -0.09375 to 0.09375
- student_up: bfloat16 [4096, 14336], P('seq', ('grp', 'tp')), may hold values from -0.09375 to 0.09375
- student_down: bfloat16 [14336, 4096], P(('grp', 'tp'), 'seq'), may hold values from -0.046875 to 0.046875
- projection: bfloat16 [4096, 8192], P('seq', ('grp', 'tp')), may hold values from -0.09375 to 0.09375
Outputs:
- grad_gate: bfloat16 [4096, 14336], P('seq', ('grp', 'tp'))
- grad_up: bfloat16 [4096, 14336], P('seq', ('grp', 'tp'))
- grad_down: bfloat16 [14336, 4096], P(('grp', 'tp'), 'seq')
- grad_proj: bfloat16 [4096, 8192], P('seq', ('grp', 'tp'))
The draws below stay inside these ranges and needn't reach their ends.
Inputs may be any that keep to these rules, and one draw needn't show every extreme that they name: `align_layer`: for each token, which of the 2 teacher layers gives its target.
All inputs are finite; a program needn't handle non-finite values.
Results may differ from the reference program's by a relative error of at most 0.013.
Values may be sent and summed in bfloat16 or wider, within the bound.
A program may use at most 64 MiB of HBM per device.

```python
import math
import jax
import jax.numpy as jnp
from jax import lax

DT = 8192
FT = 14336
DS = 4096
FS = 14336
LT = 2
TOKENS = 256


def set_ends(values, key, least, high):
    extent = values.shape
    index_at = [jax.random.randint(jax.random.fold_in(key, axis), (), 0, extent[axis]) for axis in range(len(extent))]
    values = values.at[tuple(index_at)].set(least)
    longest = extent.index(max(extent))
    index_at[longest] = (index_at[longest] + 1) % extent[longest]
    return values.at[tuple(index_at)].set(high)


def steps_of(rng, shape, pieces, low, largest):
    level, own = 1.0, jax.random.fold_in(rng, 6)
    for dim, blocks in pieces:
        steps = jnp.exp(jax.random.uniform(jax.random.fold_in(own, dim), (blocks,), jnp.float32, low / len(pieces), largest / len(pieces)))
        level = level * jnp.repeat(steps, shape[dim] // blocks).reshape([-1 if axis == dim else 1 for axis in range(len(shape))])
    return level


def gaussian(own_key, shape, deviation, reach, pieces=(), held_as=jnp.bfloat16):
    array = deviation * jax.random.normal(own_key, shape, jnp.float32)
    if pieces:
        array = array * steps_of(own_key, shape, pieces, -0.22, 0.18)
    return jnp.clip(array, -reach, reach).astype(held_as)


def setup_inputs(seed: int = 0) -> dict:
    seeds = jax.random.split(jax.random.key(seed), 13)
    return {
        "teacher_in": gaussian(seeds[0], (TOKENS, DT), 1.0, 6.0, ((1, 16),)),
        "teacher_gain": jnp.clip(1.0 + 0.18 * jax.random.normal(seeds[1], (DT,), jnp.float32), 0.1, 1.9),
        "teacher_gate": gaussian(seeds[2], (LT, DT, FT), DT ** -0.5, 0.0625, ((1, 16), (2, 16))),
        "teacher_up": gaussian(seeds[3], (LT, DT, FT), DT ** -0.5, 0.0625, ((1, 16), (2, 16))),
        "teacher_down": gaussian(seeds[4], (LT, FT, DT), FT ** -0.5, 0.046875, ((1, 16), (2, 16))),
        "align_layer": set_ends(jax.random.randint(seeds[5], (TOKENS,), 0, LT), jax.random.fold_in(seeds[5], 1), 0, LT - 1).astype(jnp.int32),
        "student_in": gaussian(seeds[6], (TOKENS, DS), 1.0, 6.0, ((1, 16),)),
        "student_gain": jnp.clip(1.0 + 0.18 * jax.random.normal(seeds[7], (DS,), jnp.float32), 0.1, 1.9),
        "student_gate": gaussian(seeds[8], (DS, FS), DS ** -0.5, 0.09375, ((0, 16), (1, 16))),
        "student_up": gaussian(seeds[9], (DS, FS), DS ** -0.5, 0.09375, ((0, 16), (1, 16))),
        "student_down": gaussian(seeds[10], (FS, DS), FS ** -0.5, 0.046875, ((0, 16), (1, 16))),
        "projection": gaussian(seeds[11], (DS, DT), DS ** -0.5, 0.09375, ((0, 16), (1, 16))),
    }


def rms_scale(values, gain, width):
    wide = values.astype(jnp.float32)
    total = lax.optimization_barrier(jnp.sum(wide * wide, axis=1, keepdims=True))
    return (wide * lax.rsqrt(total / width + 1e-05) * gain).astype(jnp.bfloat16)

def reference(teacher_in, teacher_gain, teacher_gate, teacher_up, teacher_down, align_layer, student_in, student_gain, student_gate, student_up, student_down, projection):
    teacher_normed = rms_scale(teacher_in, teacher_gain, DT)
    target = teacher_in.astype(jnp.float32)
    for layer in range(LT):
        teacher_g = jnp.dot(teacher_normed, teacher_gate[layer], preferred_element_type=jnp.float32)
        teacher_u = jnp.dot(teacher_normed, teacher_up[layer], preferred_element_type=jnp.float32)
        teacher_h = (jax.nn.silu(teacher_g) * teacher_u).astype(jnp.bfloat16)
        teacher_out = jnp.dot(teacher_h, teacher_down[layer], preferred_element_type=jnp.float32)
        target = target + jnp.where((align_layer == layer)[:, None], teacher_out, jnp.float32(0.0))
    student_normed = rms_scale(student_in, student_gain, DS)
    student_g = jnp.dot(student_normed, student_gate, preferred_element_type=jnp.float32)
    student_u = jnp.dot(student_normed, student_up, preferred_element_type=jnp.float32)
    student_h = (jax.nn.silu(student_g) * student_u).astype(jnp.bfloat16)
    state = (student_in.astype(jnp.float32) + jnp.dot(student_h, student_down, preferred_element_type=jnp.float32)).astype(jnp.bfloat16)
    pred = jnp.dot(state, projection, preferred_element_type=jnp.float32)
    d_pred = ((pred - target) / math.sqrt(TOKENS)).astype(jnp.bfloat16)
    grad_proj = jnp.dot(state.T, d_pred, preferred_element_type=jnp.float32).astype(jnp.bfloat16)
    d_state = jnp.dot(d_pred, projection.T, preferred_element_type=jnp.float32).astype(jnp.bfloat16)
    grad_down = jnp.dot(student_h.T, d_state, preferred_element_type=jnp.float32).astype(jnp.bfloat16)
    d_hidden = jnp.dot(d_state, student_down.T, preferred_element_type=jnp.float32)
    sigmoid_gate = jax.nn.sigmoid(student_g)
    d_up = (d_hidden * student_g * sigmoid_gate).astype(jnp.bfloat16)
    d_gate = (d_hidden * student_u * sigmoid_gate * (1.0 + student_g * (1.0 - sigmoid_gate))).astype(jnp.bfloat16)
    grad_gate = jnp.dot(student_normed.T, d_gate, preferred_element_type=jnp.float32).astype(jnp.bfloat16)
    grad_up = jnp.dot(student_normed.T, d_up, preferred_element_type=jnp.float32).astype(jnp.bfloat16)
    return (grad_gate, grad_up, grad_down, grad_proj)
```

```python
import functools
import math

import jax
import jax.numpy as jnp
from jax import lax
from jax.experimental import pallas as pl
from jax.experimental.pallas import tpu as pltpu
from jax.sharding import PartitionSpec as P

MESH = pl.DeviceIdType.MESH
BF = jnp.bfloat16
F32 = jnp.float32

T = 256
DT = 8192
DS = 4096
KT = 512
KS = 256
N = 896
W2 = 2 * N
WS = W2 + 128

GOFF = [
    (a, b, c) for b in (1, 3, 2, 0) for a in (0, 1) for c in (0, 1) if (a, b, c) != (0, 0, 0)
]


def dot(a, b):
    return lax.dot_general(a, b, (((1,), (0,)), ((), ())), preferred_element_type=F32)


def dot_nt(a, b):
    return lax.dot_general(a, b, (((1,), (1,)), ((), ())), preferred_element_type=F32)


class Sems:
    def __init__(self, send, recv):
        self.send, self.recv, self.used = send, recv, 0

    def copy(self, src, dst, device):
        index = self.used
        self.used += 1
        return pltpu.make_async_remote_copy(
            src_ref=src,
            dst_ref=dst,
            send_sem=self.send.at[index],
            recv_sem=self.recv.at[index],
            device_id=device,
            device_id_type=MESH,
        )


def squares(total):
    rows = total.shape[0]
    wide = jnp.broadcast_to(total, (rows, 128))
    high = wide.astype(BF)
    low = (wide - high.astype(F32)).astype(BF)
    lane = lax.broadcasted_iota(jnp.int32, (rows, 128), 1)
    return jnp.where(lane < 64, high.astype(F32), low.astype(F32)).astype(BF)


def total_of(columns):
    lane = lax.broadcasted_iota(jnp.int32, columns.shape, 1)
    picked = jnp.where((lane == 0) | (lane == 64), columns, 0.0)
    return jnp.sum(picked, axis=1, keepdims=True)


def kernel(
    t_in_h, t_gain_h, t_gate_h, t_up_h, t_down_h, align_h,
    s_in_h, s_gain_h, s_gate_h, s_up_h, s_down_h, proj_h,
    o_gate_h, o_up_h, o_down_h, o_proj_h,
    t_in, t_gain, t_w, t_down, align,
    s_in, s_gain, s_w, s_down, proj,
    xg, xt, hm, h_t,
    pb, rby, zb, rbz, own_g, own_u, own_r, h_s,
    pc, rc, pd, rd, state, tpart,
    pe, rey, ze, rez, dp, pf, rf, dst,
    pg, rgy, zg, rgz, dgu,
    o_gu, o_down, o_proj,
    send, recv, lsem,
):
    grp, seq, tp = lax.axis_index("grp"), lax.axis_index("seq"), lax.axis_index("tp")
    zh, y = seq // 4, seq % 4
    x, core = tp // 2, tp % 2

    def s_dev(dz, dy):
        return (grp, ((zh + dz) % 4) * 4 + (y + dy) % 4, tp)

    def g_dev(a, b, c):
        return ((grp + a) % 2, seq, ((x + b) % 4) * 2 + (core + c) % 2)

    def g_rows(a=0, b=0, c=0):
        owner = ((grp + a) % 2) * 8 + ((x + b) % 4) * 2 + (core + c) % 2
        return pl.ds(pl.multiple_of(owner * 16, 16), 16)

    def y_rows(dy=0):
        return pl.ds(pl.multiple_of(((y + dy) % 4) * 64, 64), 64)

    def z_rows(dz=0):
        return pl.ds(pl.multiple_of(((zh + dz) % 4) * 16, 16), 16)

    def s_rows():
        return pl.ds(pl.multiple_of(y * 64 + zh * 16, 16), 16)

    sems = Sems(send, recv)
    loads = []

    def load(src, dst):
        copy = pltpu.make_async_copy(src, dst, lsem.at[len(loads)])
        copy.start()
        loads.append(copy)
        return copy

    l_s = [
        load(s_in_h, s_in),
        load(s_gain_h, s_gain),
        load(s_gate_h, s_w.at[:, pl.ds(0, N)]),
        load(s_up_h, s_w.at[:, pl.ds(N, N)]),
    ]
    l_t = [load(t_in_h, t_in), load(t_gain_h, t_gain), load(align_h, align)]
    for layer in range(2):
        rows = pl.ds(layer * KT, KT)
        l_t.append(load(t_gate_h.at[layer], t_w.at[rows, pl.ds(0, N)]))
        l_t.append(load(t_up_h.at[layer], t_w.at[rows, pl.ds(N, N)]))
    l_sd = load(s_down_h, s_down)
    l_td = load(t_down_h, t_down)
    l_p = load(proj_h, proj)

    barrier = pltpu.get_barrier_semaphore()
    partners = [s_dev(0, k) for k in (1, 2, 3)] + [s_dev(k, 0) for k in (1, 2, 3)]
    partners += [g_dev(*o) for o in GOFF]
    for device in partners:
        pl.semaphore_signal(barrier, inc=1, device_id=device, device_id_type=MESH)

    def rs_y(src, slots):
        copies = [
            sems.copy(src.at[y_rows(k)], slots.at[k - 1], s_dev(0, k)) for k in (1, 3, 2)
        ]
        for copy in copies:
            copy.start()
        return copies

    def rs_z(src, slots):
        copies = [
            sems.copy(src.at[z_rows(k)], slots.at[k - 1], s_dev(k, 0)) for k in (1, 3, 2)
        ]
        for copy in copies:
            copy.start()
        return copies

    def ag_z(buf):
        copies = [sems.copy(buf.at[s_rows()], buf.at[s_rows()], s_dev(k, 0)) for k in (1, 3, 2)]
        for copy in copies:
            copy.start()
        return copies

    def ag_y(buf):
        copies = [sems.copy(buf.at[y_rows()], buf.at[y_rows()], s_dev(0, k)) for k in (1, 3, 2)]
        for copy in copies:
            copy.start()
        return copies

    def rs_g(src, slots):
        copies = [
            sems.copy(src.at[g_rows(*o)], slots.at[i], g_dev(*o)) for i, o in enumerate(GOFF)
        ]
        for copy in copies:
            copy.start()
        return copies

    def ag_g(buf):
        copies = [sems.copy(buf.at[g_rows()], buf.at[g_rows()], g_dev(*o)) for o in GOFF]
        for copy in copies:
            copy.start()
        return copies

    def arrived(copies):
        for copy in copies:
            copy.wait_recv()

    sent = []

    def summed(src, rows, slots, count, columns=None):
        columns = slice(None) if columns is None else columns
        total = src[rows, columns].astype(F32)
        for index in range(count):
            total = total + slots[index, :, columns].astype(F32)
        return total

    for copy in l_s:
        copy.wait()
    wide = s_in[...].astype(F32)
    xg[...] = (wide * s_gain[...]).astype(BF)
    pb[:, W2:] = squares(jnp.sum(wide * wide, axis=1, keepdims=True))
    for tile in range(7):
        cols = pl.ds(tile * 256, 256)
        pb[:, cols] = dot(xg[...], s_w[:, cols]).astype(BF)

    pl.semaphore_wait(barrier, len(partners))
    b_y = rs_y(pb, rby)

    for copy in l_t:
        copy.wait()
    diagonal = lax.broadcasted_iota(jnp.int32, (T, T), 0) == lax.broadcasted_iota(
        jnp.int32, (T, T), 1
    )
    layer_of = jnp.sum(
        jnp.where(diagonal, jnp.broadcast_to(align[...].astype(F32), (T, T)), 0.0),
        axis=1,
        keepdims=True,
    )
    hm[...] = jnp.broadcast_to(layer_of, (T, 128))
    wide = t_in[...].astype(F32)
    scaled = wide * t_gain[...]
    xt[:, :KT] = jnp.where(layer_of < 0.5, scaled, 0.0).astype(BF)
    xt[:, KT:] = jnp.where(layer_of < 0.5, 0.0, scaled).astype(BF)
    pc[:, W2:] = squares(jnp.sum(wide * wide, axis=1, keepdims=True))

    @pl.loop(0, 7)
    def _(tile):
        cols = pl.ds(pl.multiple_of(tile * 256, 256), 256)
        pc[:, cols] = dot(xt[...], t_w[:, cols]).astype(BF)

    c_rs = rs_g(pc, rc)

    arrived(b_y)
    zb[:, :W2] = summed(pb, y_rows(), rby, 3, pl.ds(0, W2)).astype(BF)
    zb[:, W2:] = squares(total_of(summed(pb, y_rows(), rby, 3, pl.ds(W2, 128))))
    b_z = rs_z(zb, rbz)

    arrived(b_z)
    total = total_of(summed(zb, z_rows(), rbz, 3, pl.ds(W2, 128)))
    scale = lax.rsqrt(total / DS + 1e-05)
    own_r[...] = jnp.broadcast_to(scale, (16, 128))
    g = summed(zb, z_rows(), rbz, 3, pl.ds(0, N)) * scale
    u = summed(zb, z_rows(), rbz, 3, pl.ds(N, N)) * scale
    own_g[...] = g
    own_u[...] = u
    h_s[s_rows(), :] = (g * jax.nn.sigmoid(g) * u).astype(BF)
    b_az = ag_z(h_s)

    arrived(c_rs)
    total = total_of(summed(pc, g_rows(), rc, 15, pl.ds(W2, 128)))
    scale = lax.rsqrt(total / DT + 1e-05)
    g = summed(pc, g_rows(), rc, 15, pl.ds(0, N)) * scale
    u = summed(pc, g_rows(), rc, 15, pl.ds(N, N)) * scale
    h_t[g_rows(), :] = (g * jax.nn.sigmoid(g) * u).astype(BF)
    c_ag = ag_g(h_t)

    arrived(b_az)
    b_ay = ag_y(h_s)
    l_sd.wait()
    l_td.wait()
    l_p.wait()
    arrived(b_ay)

    pd[...] = dot(h_s[...], s_down[...]).astype(BF)
    d_rs = rs_g(pd, rd)

    arrived(c_ag)
    first = hm[:, 0:1] < 0.5
    zero = jnp.zeros((), BF)
    for half in range(2):
        cols = pl.ds(half * 256, 256)
        tpart[:, cols] = dot(jnp.where(first, h_t[...], zero), t_down[:N, cols]) + dot(
            jnp.where(first, zero, h_t[...]), t_down[N:, cols]
        )

    arrived(d_rs)
    state[g_rows(), :] = (
        s_in[g_rows(), :].astype(F32) + summed(pd, g_rows(), rd, 15)
    ).astype(BF)
    d_ag = ag_g(state)
    arrived(d_ag)

    for half in range(2):
        cols = pl.ds(half * 256, 256)
        pe[:, cols] = (dot(state[...], proj[:, cols]) - tpart[:, cols]).astype(BF)
    e_y = rs_y(pe, rey)
    arrived(e_y)
    ze[...] = summed(pe, y_rows(), rey, 3).astype(BF)
    e_z = rs_z(ze, rez)
    arrived(e_z)
    dp[s_rows(), :] = (
        (summed(ze, z_rows(), rez, 3) - t_in[s_rows(), :].astype(F32)) * (1.0 / math.sqrt(T))
    ).astype(BF)
    e_az = ag_z(dp)
    arrived(e_az)
    e_ay = ag_y(dp)
    arrived(e_ay)

    pf[...] = dot_nt(dp[...], proj[...]).astype(BF)
    f_rs = rs_g(pf, rf)
    o_proj[...] = dot(state[...].T, dp[...]).astype(BF)
    stores = []

    def store(src, dst):
        copy = pltpu.make_async_copy(src, dst, lsem.at[len(loads) + len(stores)])
        copy.start()
        stores.append(copy)

    store(o_proj, o_proj_h)
    arrived(f_rs)
    dst[g_rows(), :] = summed(pf, g_rows(), rf, 15).astype(BF)
    f_ag = ag_g(dst)
    arrived(f_ag)

    pg[...] = dot_nt(dst[...], s_down[...]).astype(BF)
    g_y = rs_y(pg, rgy)
    o_down[...] = dot(h_s[...].T, dst[...]).astype(BF)
    store(o_down, o_down_h)
    arrived(g_y)
    zg[...] = summed(pg, y_rows(), rgy, 3).astype(BF)
    g_z = rs_z(zg, rgz)
    arrived(g_z)
    dh = summed(zg, z_rows(), rgz, 3) * own_r[:, 0:1]
    g = own_g[...]
    q = jax.nn.sigmoid(g)
    dgu[s_rows(), :N] = (dh * own_u[...] * q * (1.0 + g * (1.0 - q))).astype(BF)
    dgu[s_rows(), N:] = (dh * g * q).astype(BF)
    g_az = ag_z(dgu)
    arrived(g_az)
    g_ay = ag_y(dgu)
    x_t = xg[...].T
    arrived(g_ay)
    for tile in range(7):
        cols = pl.ds(tile * 256, 256)
        o_gu[:, cols] = dot(x_t, dgu[:, cols]).astype(BF)
    store(o_gu.at[:, pl.ds(0, N)], o_gate_h)
    store(o_gu.at[:, pl.ds(N, N)], o_up_h)

    for group in (b_y, c_rs, b_z, b_az, c_ag, b_ay, d_rs, d_ag, e_y, e_z, e_az, e_ay, f_rs,
                  f_ag, g_y, g_z, g_az, g_ay):
        for copy in group:
            copy.wait_send()
    for copy in stores:
        copy.wait()


N_REMOTE = 12 * 3 + 6 * 15
N_LOCAL = 14 + 4


def per_device(
    teacher_in, teacher_gain, teacher_gate, teacher_up, teacher_down, align_layer,
    student_in, student_gain, student_gate, student_up, student_down, projection,
):
    any_space = pl.BlockSpec(memory_space=pl.ANY)
    v = pltpu.VMEM
    scratch = [
        v((T, KT), BF), v((1, KT), F32), v((2 * KT, W2), BF), v((2 * N, KT), BF), v((1, T), jnp.int32),
        v((T, KS), BF), v((1, KS), F32), v((KS, W2), BF), v((N, KS), BF), v((KS, KT), BF),
        v((T, KS), BF), v((T, 2 * KT), BF), v((T, 128), F32), v((T, N), BF),
        v((T, WS), BF), v((3, 64, WS), BF), v((64, WS), BF), v((3, 16, WS), BF),
        v((16, N), F32), v((16, N), F32), v((16, 128), F32), v((T, N), BF),
        v((T, WS), BF), v((15, 16, WS), BF), v((T, KS), BF), v((15, 16, KS), BF),
        v((T, KS), BF), v((T, KT), F32),
        v((T, KT), BF), v((3, 64, KT), BF), v((64, KT), BF), v((3, 16, KT), BF), v((T, KT), BF),
        v((T, KS), BF), v((15, 16, KS), BF), v((T, KS), BF),
        v((T, N), BF), v((3, 64, N), BF), v((64, N), BF), v((3, 16, N), BF), v((T, W2), BF),
        v((KS, W2), BF), v((N, KS), BF), v((KS, KT), BF),
        pltpu.SemaphoreType.DMA((N_REMOTE,)),
        pltpu.SemaphoreType.DMA((N_REMOTE,)),
        pltpu.SemaphoreType.DMA((N_LOCAL,)),
    ]
    out = [
        jax.ShapeDtypeStruct((KS, N), BF),
        jax.ShapeDtypeStruct((KS, N), BF),
        jax.ShapeDtypeStruct((N, KS), BF),
        jax.ShapeDtypeStruct((KS, KT), BF),
    ]
    return pl.pallas_call(
        kernel,
        name="distill",
        out_shape=out,
        in_specs=[any_space] * 12,
        out_specs=[any_space] * 4,
        scratch_shapes=scratch,
        cost_estimate=pl.CostEstimate(flops=3 * 10**9, bytes_accessed=10**7, transcendentals=10**5),
        compiler_params=pltpu.CompilerParams(
            collective_id=0, has_side_effects=True, vmem_limit_bytes=48 * 2**20
        ),
    )(
        teacher_in, teacher_gain.reshape(1, KT), teacher_gate, teacher_up,
        teacher_down.reshape(2 * N, KT), align_layer.reshape(1, T),
        student_in, student_gain.reshape(1, KS), student_gate, student_up, student_down, projection,
    )


def solution(mesh):
    in_specs = (
        P(None, ("grp", "tp")),
        P(("grp", "tp")),
        P(None, ("grp", "tp"), "seq"),
        P(None, ("grp", "tp"), "seq"),
        P(None, "seq", ("grp", "tp")),
        P(),
        P(None, "seq"),
        P("seq"),
        P("seq", ("grp", "tp")),
        P("seq", ("grp", "tp")),
        P(("grp", "tp"), "seq"),
        P("seq", ("grp", "tp")),
    )
    out_specs = (
        P("seq", ("grp", "tp")),
        P("seq", ("grp", "tp")),
        P(("grp", "tp"), "seq"),
        P("seq", ("grp", "tp")),
    )
    return jax.shard_map(
        per_device, mesh=mesh, in_specs=in_specs, out_specs=out_specs, check_vma=False
    )
```

```python
import functools
import math

import jax
import jax.numpy as jnp
from jax import lax
from jax.experimental import pallas as pl
from jax.experimental.pallas import tpu as pltpu
from jax.sharding import PartitionSpec as P

MESH = pl.DeviceIdType.MESH
BF = jnp.bfloat16
F32 = jnp.float32

T = 256
DT = 8192
DS = 4096
KT = 512
KS = 256
N = 896
W2 = 2 * N
WS = W2 + 128

GOFF = [
    (a, b, c) for b in (1, 3, 2, 0) for a in (0, 1) for c in (0, 1) if (a, b, c) != (0, 0, 0)
]


def dot(a, b):
    return lax.dot_general(a, b, (((1,), (0,)), ((), ())), preferred_element_type=F32)


def dot_nt(a, b):
    return lax.dot_general(a, b, (((1,), (1,)), ((), ())), preferred_element_type=F32)


class Sems:
    def __init__(self, send, recv):
        self.send, self.recv, self.started = send, recv, []

    def start(self, src, dst, device):
        index = len(self.started)
        copy = pltpu.make_async_remote_copy(
            src_ref=src,
            dst_ref=dst,
            send_sem=self.send.at[index],
            recv_sem=self.recv.at[index],
            device_id=device,
            device_id_type=MESH,
        )
        copy.start()
        self.started.append(copy)
        return copy


def squares(total):
    rows = total.shape[0]
    wide = jnp.broadcast_to(total, (rows, 128))
    high = wide.astype(BF)
    low = (wide - high.astype(F32)).astype(BF)
    lane = lax.broadcasted_iota(jnp.int32, (rows, 128), 1)
    return jnp.where(lane < 64, high.astype(F32), low.astype(F32)).astype(BF)


def total_of(columns):
    lane = lax.broadcasted_iota(jnp.int32, columns.shape, 1)
    picked = jnp.where((lane == 0) | (lane == 64), columns, 0.0)
    return jnp.sum(picked, axis=1, keepdims=True)


def kernel(
    t_in_h, t_gain_h, t_gate_h, t_up_h, t_down_h, align_h,
    s_in_h, s_gain_h, s_gate_h, s_up_h, s_down_h, proj_h,
    xt_h, dgu_h, o_down_h, o_proj_h,
    t_in, t_gain, t_w, t_down, align,
    s_in, s_gain, s_w, s_down, proj,
    xg, xgt, xt, hm, h_t,
    pb, rby, zb, rbz, h_s, coef,
    pc, rc, pd, rd, state, tpart,
    pe, rey, ze, rez, dp, pf, rf, d_state,
    pg, rgy, zg, rgz, dh, dgu,
    o_down, o_proj,
    send, recv, lsem,
):
    grp, seq, tp = lax.axis_index("grp"), lax.axis_index("seq"), lax.axis_index("tp")
    zh, y = seq // 4, seq % 4
    x, core = tp // 2, tp % 2

    def s_dev(dz, dy):
        return (grp, ((zh + dz) % 4) * 4 + (y + dy) % 4, tp)

    def g_dev(a, b, c):
        return ((grp + a) % 2, seq, ((x + b) % 4) * 2 + (core + c) % 2)

    def g_rows(a=0, b=0, c=0):
        owner = ((grp + a) % 2) * 8 + ((x + b) % 4) * 2 + (core + c) % 2
        return pl.ds(pl.multiple_of(owner * 16, 16), 16)

    def s_rows(dz=0, dy=0):
        owner = ((y + dy) % 4) * 4 + (zh + dz) % 4
        return pl.ds(pl.multiple_of(owner * 16, 16), 16)

    sems = Sems(send, recv)
    loads = []

    def load(src, dst):
        copy = pltpu.make_async_copy(src, dst, lsem.at[len(loads)])
        copy.start()
        loads.append(copy)
        return copy

    l_s = [
        load(s_in_h, s_in),
        load(s_gain_h, s_gain),
        load(s_gate_h, s_w.at[:, pl.ds(0, N)]),
        load(s_up_h, s_w.at[:, pl.ds(N, N)]),
    ]
    l_t = [load(t_in_h, t_in), load(t_gain_h, t_gain), load(align_h, align)]
    for layer in range(2):
        rows = pl.ds(layer * KT, KT)
        l_t.append(load(t_gate_h.at[layer], t_w.at[rows, pl.ds(0, N)]))
        l_t.append(load(t_up_h.at[layer], t_w.at[rows, pl.ds(N, N)]))
    l_sd = load(s_down_h, s_down)
    l_td = load(t_down_h, t_down)
    l_p = load(proj_h, proj)

    barrier = pltpu.get_barrier_semaphore()
    partners = [s_dev(0, k) for k in (1, 2, 3)] + [s_dev(k, 0) for k in (1, 2, 3)]
    partners += [g_dev(*o) for o in GOFF]
    for device in partners:
        pl.semaphore_signal(barrier, inc=1, device_id=device, device_id_type=MESH)

    def arrived(copies):
        for copy in copies:
            copy.wait_recv()

    def rs_start(src, slots):
        return {
            dz: [
                sems.start(src.at[s_rows(dz, dy)], slots.at[dz, dy - 1], s_dev(0, dy))
                for dy in (2, 1, 3)
            ]
            for dz in (2, 1, 3, 0)
        }

    def y_sum(src, slots, dz, columns=slice(None)):
        total = src[s_rows(dz), columns].astype(F32)
        for index in range(3):
            total = total + slots[dz, index, :, columns].astype(F32)
        return total

    def rs_pass(copies, src, slots, held, slots_z, fill):
        onward = []
        for dz in (2, 1, 3):
            arrived(copies[dz])
            fill(held, dz, src, slots)
            onward.append(sems.start(held.at[dz - 1], slots_z.at[dz - 1], s_dev(dz, 0)))
        arrived(copies[0])
        return onward

    def fill_plain(held, dz, src, slots):
        held[dz - 1] = y_sum(src, slots, dz).astype(BF)

    def fill_squares(held, dz, src, slots):
        held[dz - 1, :, :W2] = y_sum(src, slots, dz, pl.ds(0, W2)).astype(BF)
        held[dz - 1, :, W2:] = squares(total_of(y_sum(src, slots, dz, pl.ds(W2, 128))))

    def rs_total(src, slots, slots_z, columns=slice(None)):
        total = y_sum(src, slots, 0, columns)
        for index in range(3):
            total = total + slots_z[index, :, columns].astype(F32)
        return total

    def ag_start(buf):
        along_z = {dz: sems.start(buf.at[s_rows()], buf.at[s_rows()], s_dev(dz, 0)) for dz in (2, 1, 3)}
        along_y = [sems.start(buf.at[s_rows()], buf.at[s_rows()], s_dev(0, dy)) for dy in (2, 1, 3)]
        return along_z, along_y

    def ag_pass(copies, buf):
        along_z, along_y = copies
        for dz in (1, 3, 2):
            arrived([along_z[dz]])
            rows = s_rows(4 - dz)
            along_y += [sems.start(buf.at[rows], buf.at[rows], s_dev(0, dy)) for dy in (2, 1, 3)]
        return along_y

    def rs_g(src, slots):
        return [
            sems.start(src.at[g_rows(*o)], slots.at[i], g_dev(*o)) for i, o in enumerate(GOFF)
        ]

    def ag_g(buf):
        return [sems.start(buf.at[g_rows()], buf.at[g_rows()], g_dev(*o)) for o in GOFF]

    def g_total(src, slots, columns=slice(None)):
        total = src[g_rows(), columns].astype(F32)
        for index in range(15):
            total = total + slots[index, :, columns].astype(F32)
        return total

    for copy in l_s:
        copy.wait()
    wide = s_in[...].astype(F32)
    xg[...] = (wide * s_gain[...]).astype(BF)
    pb[:, W2:] = squares(jnp.sum(wide * wide, axis=1, keepdims=True))
    for tile in range(7):
        cols = pl.ds(tile * 256, 256)
        pb[:, cols] = dot(xg[...], s_w[:, cols]).astype(BF)

    pl.semaphore_wait(barrier, len(partners))
    b_y = rs_start(pb, rby)

    for copy in l_t:
        copy.wait()
    diagonal = lax.broadcasted_iota(jnp.int32, (T, T), 0) == lax.broadcasted_iota(
        jnp.int32, (T, T), 1
    )
    layer_of = jnp.sum(
        jnp.where(diagonal, jnp.broadcast_to(align[...].astype(F32), (T, T)), 0.0),
        axis=1,
        keepdims=True,
    )
    hm[...] = jnp.broadcast_to(layer_of, (T, 128))
    wide = t_in[...].astype(F32)
    scaled = wide * t_gain[...]
    xt[:, :KT] = jnp.where(layer_of < 0.5, scaled, 0.0).astype(BF)
    xt[:, KT:] = jnp.where(layer_of < 0.5, 0.0, scaled).astype(BF)
    pc[:, W2:] = squares(jnp.sum(wide * wide, axis=1, keepdims=True))

    @pl.loop(0, 7)
    def _(tile):
        cols = pl.ds(pl.multiple_of(tile * 256, 256), 256)
        pc[:, cols] = dot(xt[...], t_w[:, cols]).astype(BF)

    c_rs = rs_g(pc, rc)
    xgt[...] = xg[...].T

    b_z = rs_pass(b_y, pb, rby, zb, rbz, fill_squares)
    arrived(b_z)
    total = total_of(rs_total(pb, rby, rbz, pl.ds(W2, 128)))
    scale = lax.rsqrt(total / DS + 1e-05)
    g = rs_total(pb, rby, rbz, pl.ds(0, N)) * scale
    u = rs_total(pb, rby, rbz, pl.ds(N, N)) * scale
    q = jax.nn.sigmoid(g)
    h_s[s_rows(), :] = (g * q * u).astype(BF)
    b_ag = ag_start(h_s)
    coef[s_rows(), :N] = (scale * u * q * (1.0 + g * (1.0 - q))).astype(BF)
    coef[s_rows(), N:] = (scale * g * q).astype(BF)
    b_ay = ag_pass(b_ag, h_s)
    k_ag = ag_start(coef)

    arrived(c_rs)
    total = total_of(g_total(pc, rc, pl.ds(W2, 128)))
    scale = lax.rsqrt(total / DT + 1e-05)
    g = g_total(pc, rc, pl.ds(0, N)) * scale
    u = g_total(pc, rc, pl.ds(N, N)) * scale
    h_t[g_rows(), :] = (g * jax.nn.sigmoid(g) * u).astype(BF)
    c_ag = ag_g(h_t)

    l_sd.wait()
    l_td.wait()
    l_p.wait()
    arrived(b_ay)

    pd[...] = dot(h_s[...], s_down[...]).astype(BF)
    d_rs = rs_g(pd, rd)
    k_ay = ag_pass(k_ag, coef)
    arrived(d_rs)
    state[g_rows(), :] = (s_in[g_rows(), :].astype(F32) + g_total(pd, rd)).astype(BF)
    d_ag = ag_g(state)

    arrived(c_ag)
    first = hm[:, 0:1] < 0.5
    zero = jnp.zeros((), BF)
    for half in range(2):
        cols = pl.ds(half * 256, 256)
        tpart[:, cols] = dot(jnp.where(first, h_t[...], zero), t_down[:N, cols]) + dot(
            jnp.where(first, zero, h_t[...]), t_down[N:, cols]
        )
    arrived(d_ag)

    for half in range(2):
        cols = pl.ds(half * 256, 256)
        pe[:, cols] = (dot(state[...], proj[:, cols]) - tpart[:, cols]).astype(BF)
    e_y = rs_start(pe, rey)
    e_z = rs_pass(e_y, pe, rey, ze, rez, fill_plain)
    arrived(e_z)
    dp[s_rows(), :] = (
        (rs_total(pe, rey, rez) - t_in[s_rows(), :].astype(F32)) * (1.0 / math.sqrt(T))
    ).astype(BF)
    e_ag = ag_start(dp)
    e_ay = ag_pass(e_ag, dp)
    arrived(e_ay)

    pf[...] = dot_nt(dp[...], proj[...]).astype(BF)
    f_rs = rs_g(pf, rf)
    o_proj[...] = dot(state[...].T, dp[...]).astype(BF)
    stores = []

    def store(src, dst):
        copy = pltpu.make_async_copy(src, dst, lsem.at[len(loads) + len(stores)])
        copy.start()
        stores.append(copy)

    store(o_proj, o_proj_h)
    store(xgt, xt_h)
    arrived(f_rs)
    d_state[g_rows(), :] = g_total(pf, rf).astype(BF)
    f_ag = ag_g(d_state)
    arrived(f_ag)

    pg[...] = dot_nt(d_state[...], s_down[...]).astype(BF)
    g_y = rs_start(pg, rgy)
    o_down[...] = dot(h_s[...].T, d_state[...]).astype(BF)
    store(o_down, o_down_h)
    g_z = rs_pass(g_y, pg, rgy, zg, rgz, fill_plain)
    arrived(g_z)
    dh[s_rows(), :] = rs_total(pg, rgy, rgz).astype(BF)
    g_ag = ag_start(dh)
    g_ay = ag_pass(g_ag, dh)
    arrived(k_ay)
    arrived(g_ay)
    for half in range(2):
        cols = pl.ds(half * N, N)
        dgu[:, cols] = (dh[...].astype(F32) * coef[:, cols].astype(F32)).astype(BF)
        store(dgu.at[:, cols], dgu_h.at[:, cols])

    for copy in sems.started:
        copy.wait_send()
    for copy in stores:
        copy.wait()


N_REMOTE = 7 * 15 + 6 * 15
N_LOCAL = 14 + 5


def results(
    xt_h, dgu_h, down_h, proj_h, o_gate_h, o_up_h, o_down_h, o_proj_h, xt, dgu, down, proj, out, sem
):
    gate, up = pl.ds(0, N), pl.ds(N, N)
    moves = [
        (xt_h, xt),
        (dgu_h.at[:, gate], dgu.at[:, gate]),
        (dgu_h.at[:, up], dgu.at[:, up]),
        (down_h, down),
        (proj_h, proj),
        (out.at[:, gate], o_gate_h),
        (out.at[:, up], o_up_h),
        (down, o_down_h),
        (proj, o_proj_h),
    ]
    copies = [
        pltpu.make_async_copy(src, dst, sem.at[index]) for index, (src, dst) in enumerate(moves)
    ]
    for copy in copies[:5]:
        copy.start()
    copies[0].wait()
    for half, cols in enumerate((gate, up)):
        copies[1 + half].wait()
        out[:, cols] = dot(xt[...], dgu[:, cols]).astype(BF)
        copies[5 + half].start()
        copies[3 + half].wait()
        copies[7 + half].start()
    for copy in copies[5:]:
        copy.wait()


def per_device(
    teacher_in, teacher_gain, teacher_gate, teacher_up, teacher_down, align_layer,
    student_in, student_gain, student_gate, student_up, student_down, projection,
):
    any_space = pl.BlockSpec(memory_space=pl.ANY)
    v = pltpu.VMEM
    scratch = [
        v((T, KT), BF), v((1, KT), F32), v((2 * KT, W2), BF), v((2 * N, KT), BF), v((1, T), jnp.int32),
        v((T, KS), BF), v((1, KS), F32), v((KS, W2), BF), v((N, KS), BF), v((KS, KT), BF),
        v((T, KS), BF), v((KS, T), BF), v((T, 2 * KT), BF), v((T, 128), F32), v((T, N), BF),
        v((T, WS), BF), v((4, 3, 16, WS), BF), v((3, 16, WS), BF), v((3, 16, WS), BF),
        v((T, N), BF), v((T, W2), BF),
        v((T, WS), BF), v((15, 16, WS), BF), v((T, KS), BF), v((15, 16, KS), BF),
        v((T, KS), BF), v((T, KT), F32),
        v((T, KT), BF), v((4, 3, 16, KT), BF), v((3, 16, KT), BF), v((3, 16, KT), BF), v((T, KT), BF),
        v((T, KS), BF), v((15, 16, KS), BF), v((T, KS), BF),
        v((T, N), BF), v((4, 3, 16, N), BF), v((3, 16, N), BF), v((3, 16, N), BF), v((T, N), BF),
        v((T, W2), BF), v((N, KS), BF), v((KS, KT), BF),
        pltpu.SemaphoreType.DMA((N_REMOTE,)),
        pltpu.SemaphoreType.DMA((N_REMOTE,)),
        pltpu.SemaphoreType.DMA((N_LOCAL,)),
    ]
    out = [
        jax.ShapeDtypeStruct((KS, T), BF),
        jax.ShapeDtypeStruct((T, W2), BF),
        jax.ShapeDtypeStruct((N, KS), BF),
        jax.ShapeDtypeStruct((KS, KT), BF),
    ]
    held = pl.pallas_call(
        kernel,
        name="distill",
        out_shape=out,
        in_specs=[any_space] * 12,
        out_specs=[any_space] * 4,
        scratch_shapes=scratch,
        cost_estimate=pl.CostEstimate(flops=3 * 10**9, bytes_accessed=10**7, transcendentals=10**5),
        compiler_params=pltpu.CompilerParams(
            collective_id=0, has_side_effects=True, vmem_limit_bytes=60 * 2**20
        ),
    )(
        teacher_in, teacher_gain.reshape(1, KT), teacher_gate, teacher_up,
        teacher_down.reshape(2 * N, KT), align_layer.reshape(1, T),
        student_in, student_gain.reshape(1, KS), student_gate, student_up, student_down, projection,
    )
    return pl.pallas_call(
        results,
        name="results",
        out_shape=[
            jax.ShapeDtypeStruct((KS, N), BF),
            jax.ShapeDtypeStruct((KS, N), BF),
            jax.ShapeDtypeStruct((N, KS), BF),
            jax.ShapeDtypeStruct((KS, KT), BF),
        ],
        in_specs=[any_space] * 4,
        out_specs=[any_space] * 4,
        scratch_shapes=[
            v((KS, T), BF), v((T, W2), BF), v((N, KS), BF), v((KS, KT), BF),
            v((KS, W2), BF), pltpu.SemaphoreType.DMA((9,)),
        ],
        cost_estimate=pl.CostEstimate(flops=3 * 10**8, bytes_accessed=4 * 10**6, transcendentals=0),
        compiler_params=pltpu.CompilerParams(vmem_limit_bytes=60 * 2**20),
    )(*held)


def solution(mesh):
    in_specs = (
        P(None, ("grp", "tp")),
        P(("grp", "tp")),
        P(None, ("grp", "tp"), "seq"),
        P(None, ("grp", "tp"), "seq"),
        P(None, "seq", ("grp", "tp")),
        P(),
        P(None, "seq"),
        P("seq"),
        P("seq", ("grp", "tp")),
        P("seq", ("grp", "tp")),
        P(("grp", "tp"), "seq"),
        P("seq", ("grp", "tp")),
    )
    out_specs = (
        P("seq", ("grp", "tp")),
        P("seq", ("grp", "tp")),
        P(("grp", "tp"), "seq"),
        P("seq", ("grp", "tp")),
    )
    return jax.shard_map(
        per_device, mesh=mesh, in_specs=in_specs, out_specs=out_specs, check_vma=False
    )
```

```python
import functools
import math

import jax
import jax.numpy as jnp
from jax import lax
from jax.experimental import pallas as pl
from jax.experimental.pallas import tpu as pltpu
from jax.sharding import PartitionSpec as P

MESH = pl.DeviceIdType.MESH
BF = jnp.bfloat16
F32 = jnp.float32

T = 256
DT = 8192
DS = 4096
KT = 512
KS = 256
N = 896
W2 = 2 * N
WS = W2 + 128

GOFF = [
    (a, b, c) for b in (1, 3, 2, 0) for a in (0, 1) for c in (0, 1) if (a, b, c) != (0, 0, 0)
]


def dot(a, b):
    return lax.dot_general(a, b, (((1,), (0,)), ((), ())), preferred_element_type=F32)


def dot_nt(a, b):
    return lax.dot_general(a, b, (((1,), (1,)), ((), ())), preferred_element_type=F32)


CHIPS = [o for o in GOFF if o[2] == 0]


class Sems:
    def __init__(self, send, recv):
        self.send, self.recv, self.started = send, recv, []

    def start(self, src, dst, device):
        index = len(self.started)
        copy = pltpu.make_async_remote_copy(
            src_ref=src,
            dst_ref=dst,
            send_sem=self.send.at[index],
            recv_sem=self.recv.at[index],
            device_id=device,
            device_id_type=MESH,
        )
        copy.start()
        self.started.append(copy)
        return copy


def squares(total):
    rows = total.shape[0]
    wide = jnp.broadcast_to(total, (rows, 128))
    high = wide.astype(BF)
    low = (wide - high.astype(F32)).astype(BF)
    lane = lax.broadcasted_iota(jnp.int32, (rows, 128), 1)
    return jnp.where(lane < 64, high.astype(F32), low.astype(F32)).astype(BF)


def total_of(columns):
    lane = lax.broadcasted_iota(jnp.int32, columns.shape, 1)
    picked = jnp.where((lane == 0) | (lane == 64), columns, 0.0)
    return jnp.sum(picked, axis=1, keepdims=True)


def kernel(
    t_in_h, t_gain_h, t_gate_h, t_up_h, t_down_h, align_h,
    s_in_h, s_gain_h, s_gate_h, s_up_h, s_down_h, proj_h,
    xt_h, dgu_h, o_down_h, o_proj_h,
    t_in, t_gain, t_w, t_down, align,
    s_in, s_gain, s_w, down, proj, s_tok,
    xg, xgt, xt, hm, h_t,
    pb, rby, zb, rbz, h_s, coef,
    pc, rcore, pcore, rc, tp, rt, pd, rd, state,
    pe, rez, dp, pf, rf, d_state,
    pg, rgz, dh, dgu, state_f, d_state_f,
    o_down, o_proj,
    send, recv, lsem,
):
    grp, seq, tpi = lax.axis_index("grp"), lax.axis_index("seq"), lax.axis_index("tp")
    zh, y = seq // 4, seq % 4
    x, core = tpi // 2, tpi % 2

    def s_dev(dz, dy):
        return (grp, ((zh + dz) % 4) * 4 + (y + dy) % 4, tpi)

    def g_dev(a, b, c):
        return ((grp + a) % 2, seq, ((x + b) % 4) * 2 + (core + c) % 2)

    def g_rows(a=0, b=0, c=0):
        owner = ((core + c) % 2) * 8 + ((grp + a) % 2) * 4 + (x + b) % 4
        return pl.ds(pl.multiple_of(owner * 16, 16), 16)

    def half_rows(c=0):
        return pl.ds(pl.multiple_of(((core + c) % 2) * 128, 128), 128)

    def g_block(a=0, b=0, c=0):
        row = ((core + c) % 2) * 2 + (grp + a) % 2
        return (
            pl.ds(pl.multiple_of(row * 16, 16), 16),
            pl.ds(pl.multiple_of(((x + b) % 4) * KS, KS), KS),
        )

    def s_rows(dz=0, dy=0):
        owner = ((y + dy) % 4) * 4 + (zh + dz) % 4
        return pl.ds(pl.multiple_of(owner * 16, 16), 16)

    def y_rows(dy=0):
        return pl.ds(pl.multiple_of(((y + dy) % 4) * 64, 64), 64)

    def z_rows(dz=0):
        return pl.ds(pl.multiple_of(((zh + dz) % 4) * 16, 16), 16)

    def feat(dy=0, start=0, count=KS):
        return pl.ds(pl.multiple_of(((y + dy) % 4) * KS + start, 128), count)

    sems = Sems(send, recv)
    loads = []

    def load(src, dst):
        copy = pltpu.make_async_copy(src, dst, lsem.at[len(loads)])
        copy.start()
        loads.append(copy)
        return copy

    def arrived(copies):
        for copy in copies:
            copy.wait_recv()

    l_s = [
        load(s_in_h, s_in),
        load(s_gain_h, s_gain),
        load(s_gate_h, s_w.at[:, pl.ds(0, N)]),
        load(s_up_h, s_w.at[:, pl.ds(N, N)]),
    ]
    barrier = pltpu.get_barrier_semaphore()
    partners = [s_dev(0, k) for k in (1, 2, 3)] + [s_dev(k, 0) for k in (1, 2, 3)]
    partners += [g_dev(*o) for o in GOFF]
    for device in partners:
        pl.semaphore_signal(barrier, inc=1, device_id=device, device_id_type=MESH)

    def y_sum(src, slots, dz, columns):
        total = src[s_rows(dz), columns].astype(F32)
        for index in range(3):
            total = total + slots[dz, index, :, columns].astype(F32)
        return total

    def rs_z(src, slots):
        return [
            sems.start(src.at[z_rows(dz)], slots.at[dz - 1], s_dev(dz, 0)) for dz in (2, 1, 3)
        ]

    def z_total(src, slots):
        total = src[z_rows(), :].astype(F32)
        for index in range(3):
            total = total + slots[index].astype(F32)
        return total

    def ag_z(buf):
        return [sems.start(buf.at[s_rows()], buf.at[s_rows()], s_dev(dz, 0)) for dz in (2, 1, 3)]

    def to_y(src, dst):
        return [sems.start(src(dy), dst(dy), s_dev(0, dy)) for dy in (2, 1, 3)]

    def ag_y(buf):
        return to_y(lambda dy: buf.at[y_rows()], lambda dy: buf.at[y_rows()])

    def rs_g(src, slots):
        return [
            sems.start(src.at[g_block(*o)], slots.at[i], g_dev(*o)) for i, o in enumerate(GOFF)
        ]

    def ag_g(buf):
        return [sems.start(buf.at[g_block()], buf.at[g_block()], g_dev(*o)) for o in GOFF]

    def g_total(src, slots):
        total = src[g_block()].astype(F32)
        for index in range(15):
            total = total + slots[index].astype(F32)
        return total

    def neighbours(src, dst):
        return [sems.start(src, dst, s_dev(0, dy)) for dy in (1, 3)]

    def proj_half(dy, half):
        return proj.at[feat(dy, half * 128, 128), :]

    def down_half(dy, half):
        return down.at[pl.ds(half * (N // 2), N // 2), feat(dy)]

    def relay(copies, part):
        arrived(copies)
        return [
            sems.start(part(3, 0), part(3, 0), s_dev(0, 1)),
            sems.start(part(1, 1), part(1, 1), s_dev(0, 3)),
        ]

    for copy in l_s[:2]:
        copy.wait()
    wide = s_in[...].astype(F32)
    xg[...] = (wide * s_gain[...]).astype(BF)
    pb[:, W2:] = squares(jnp.sum(wide * wide, axis=1, keepdims=True))
    for copy in l_s[2:]:
        copy.wait()
    l_t = [load(t_in_h, t_in), load(t_gain_h, t_gain), load(align_h, align)]
    for layer in range(2):
        rows = pl.ds(layer * KT, KT)
        l_t.append(load(t_gate_h.at[layer], t_w.at[rows, pl.ds(0, N)]))
        l_t.append(load(t_up_h.at[layer], t_w.at[rows, pl.ds(N, N)]))
    l_sd = load(s_down_h, down.at[:, feat()])
    l_p = load(proj_h, proj.at[feat(), :])
    l_td = load(t_down_h, t_down)
    for tile in range(7):
        cols = pl.ds(tile * 256, 256)
        pb[:, cols] = dot(xg[...], s_w[:, cols]).astype(BF)

    pl.semaphore_wait(barrier, len(partners))
    b_y = {
        dz: [
            sems.start(pb.at[s_rows(dz, dy)], rby.at[dz, dy - 1], s_dev(0, dy))
            for dy in (2, 1, 3)
        ]
        for dz in (2, 1, 3, 0)
    }

    for copy in l_t:
        copy.wait()
    diagonal = lax.broadcasted_iota(jnp.int32, (T, T), 0) == lax.broadcasted_iota(
        jnp.int32, (T, T), 1
    )
    layer_of = jnp.sum(
        jnp.where(diagonal, jnp.broadcast_to(align[...].astype(F32), (T, T)), 0.0),
        axis=1,
        keepdims=True,
    )
    hm[...] = jnp.broadcast_to(layer_of, (T, 128))
    wide = t_in[...].astype(F32)
    scaled = wide * t_gain[...]
    xt[:, :KT] = jnp.where(layer_of < 0.5, scaled, 0.0).astype(BF)
    xt[:, KT:] = jnp.where(layer_of < 0.5, 0.0, scaled).astype(BF)
    pc[:, W2:] = squares(jnp.sum(wide * wide, axis=1, keepdims=True))

    @pl.loop(0, 7)
    def _(tile):
        cols = pl.ds(pl.multiple_of(tile * 256, 256), 256)
        pc[:, cols] = dot(xt[...], t_w[:, cols]).astype(BF)

    c_core = sems.start(pc.at[half_rows(1)], rcore, g_dev(0, 0, 1))
    xgt[...] = xg[...].T
    l_sd.wait()
    l_p.wait()
    arrived([c_core])
    pair = pc[half_rows(), :W2].astype(F32) + rcore[:, :W2].astype(F32)
    pcore[half_rows(), :W2] = pair.astype(BF)
    pair = total_of(pc[half_rows(), W2:].astype(F32) + rcore[:, W2:].astype(F32))
    pcore[half_rows(), W2:] = squares(pair)
    c_rs = [sems.start(pcore.at[g_rows(*o)], rc.at[i], g_dev(*o)) for i, o in enumerate(CHIPS)]

    def c_total(columns):
        total = pcore[g_rows(), columns].astype(F32)
        for index in range(7):
            total = total + rc[index, :, columns].astype(F32)
        return total

    b_z = []
    for dz in (2, 1, 3):
        arrived(b_y[dz])
        zb[dz - 1, :, :W2] = y_sum(pb, rby, dz, pl.ds(0, W2)).astype(BF)
        zb[dz - 1, :, W2:] = squares(total_of(y_sum(pb, rby, dz, pl.ds(W2, 128))))
        b_z.append(sems.start(zb.at[dz - 1], rbz.at[dz - 1], s_dev(dz, 0)))
    arrived(b_y[0])
    w_down = neighbours(down.at[:, feat()], down.at[:, feat()])
    w_proj = neighbours(proj.at[feat(), :], proj.at[feat(), :])
    w_tok = to_y(lambda dy: s_in.at[y_rows(dy)], lambda dy: s_tok.at[:, feat()])
    s_tok[:, feat()] = s_in[y_rows(), :]

    def b_total(columns):
        total = y_sum(pb, rby, 0, columns)
        for index in range(3):
            total = total + rbz[index, :, columns].astype(F32)
        return total

    arrived(b_z)
    scale = lax.rsqrt(total_of(b_total(pl.ds(W2, 128))) / DS + 1e-05)
    g = b_total(pl.ds(0, N)) * scale
    u = b_total(pl.ds(N, N)) * scale
    q = jax.nn.sigmoid(g)
    h_s[s_rows(), :] = (g * q * u).astype(BF)
    b_ag = ag_z(h_s)
    coef[s_rows(), :N] = (scale * u * q * (1.0 + g * (1.0 - q))).astype(BF)
    coef[s_rows(), N:] = (scale * g * q).astype(BF)

    arrived(c_rs)
    scale = lax.rsqrt(total_of(c_total(pl.ds(W2, 128))) / DT + 1e-05)
    g = c_total(pl.ds(0, N)) * scale
    u = c_total(pl.ds(N, N)) * scale
    h_t[g_rows(), :] = (g * jax.nn.sigmoid(g) * u).astype(BF)
    c_ag = [sems.start(h_t.at[g_rows()], h_t.at[g_rows()], g_dev(*o)) for o in CHIPS]

    w_down += relay(w_down, down_half)
    arrived(c_ag)
    c_core = sems.start(h_t.at[half_rows()], h_t.at[half_rows()], g_dev(0, 0, 1))
    w_proj += relay(w_proj, proj_half)
    arrived(b_ag)
    arrived(w_down[2:])

    for tile in range(4):
        cols = pl.ds(tile * 256, 256)
        pd[:, cols] = dot(h_s[y_rows(), :], down[:, cols]).astype(BF)
    d_rs = rs_g(pd, rd)

    l_td.wait()
    arrived([c_core])
    first = hm[:, 0:1] < 0.5
    zero = jnp.zeros((), BF)
    for half in range(2):
        cols = pl.ds(half * 256, 256)
        tp[:, cols] = (
            dot(jnp.where(first, h_t[...], zero), t_down[:N, cols])
            + dot(jnp.where(first, zero, h_t[...]), t_down[N:, cols])
        ).astype(BF)
    t_rs = to_y(lambda dy: tp.at[y_rows(dy)], lambda dy: rt.at[dy - 1])

    arrived(w_tok)
    arrived(d_rs)
    state[g_block()] = (s_tok[g_block()].astype(F32) + g_total(pd, rd)).astype(BF)
    d_ag = ag_g(state)
    k_ag = ag_z(coef)
    h_ag = ag_y(h_s)
    arrived(w_proj[2:])
    arrived(t_rs)
    arrived(d_ag)

    for half in range(2):
        cols = pl.ds(half * 256, 256)
        target = tp[y_rows(), cols].astype(F32)
        for index in range(3):
            target = target + rt[index, :, cols].astype(F32)
        pe[:, cols] = (dot(state[...], proj[:, cols]) - target).astype(BF)
    e_z = rs_z(pe, rez)
    s_aa = to_y(lambda dy: state.at[:, feat(dy)], lambda dy: state_f.at[y_rows()])
    state_f[y_rows(), :] = state[:, feat()]
    arrived(e_z)
    dp[s_rows(), :] = (
        (z_total(pe, rez) - t_in[s_rows(), :].astype(F32)) * (1.0 / math.sqrt(T))
    ).astype(BF)
    e_ag = ag_z(dp)
    arrived(k_ag)
    k_ay = ag_y(coef)
    arrived(e_ag)

    for tile in range(4):
        cols = pl.ds(tile * 256, 256)
        pf[:, cols] = dot_nt(dp[y_rows(), :], proj[cols, :]).astype(BF)
    f_rs = rs_g(pf, rf)
    p_ag = ag_y(dp)
    arrived(f_rs)
    d_state[g_block()] = g_total(pf, rf).astype(BF)
    f_ag = ag_g(d_state)
    stores = []

    def store(src, dst):
        copy = pltpu.make_async_copy(src, dst, lsem.at[len(loads) + len(stores)])
        copy.start()
        stores.append(copy)

    store(xgt, xt_h)
    arrived(s_aa)
    state_t = state_f[...].T
    arrived(f_ag)

    pg[...] = dot_nt(d_state[...], down[...]).astype(BF)
    g_z = rs_z(pg, rgz)
    d_aa = to_y(lambda dy: d_state.at[:, feat(dy)], lambda dy: d_state_f.at[y_rows()])
    d_state_f[y_rows(), :] = d_state[:, feat()]
    arrived(p_ag)
    o_proj[...] = dot(state_t, dp[...]).astype(BF)
    store(o_proj, o_proj_h)
    arrived(g_z)
    dh[s_rows(), :] = z_total(pg, rgz).astype(BF)
    g_az = {dz: sems.start(dh.at[s_rows()], dh.at[s_rows()], s_dev(dz, 0)) for dz in (2, 1, 3)}
    g_ay = [sems.start(dh.at[s_rows()], dh.at[s_rows()], s_dev(0, dy)) for dy in (2, 1, 3)]
    arrived(h_ag)
    arrived(d_aa)
    o_down[...] = dot(h_s[...].T, d_state_f[...]).astype(BF)
    store(o_down, o_down_h)
    for dz in (1, 3, 2):
        arrived([g_az[dz]])
        rows = s_rows(4 - dz)
        g_ay += [sems.start(dh.at[rows], dh.at[rows], s_dev(0, dy)) for dy in (2, 1, 3)]
    arrived(k_ay)
    arrived(g_ay)
    for half in range(2):
        cols = pl.ds(half * N, N)
        dgu[:, cols] = (dh[...].astype(F32) * coef[:, cols].astype(F32)).astype(BF)
        store(dgu.at[:, cols], dgu_h.at[:, cols])

    for copy in sems.started:
        copy.wait_send()
    for copy in stores:
        copy.wait()


N_REMOTE = 160
N_LOCAL = 14 + 5


def results(
    xt_h, dgu_h, down_h, proj_h, o_gate_h, o_up_h, o_down_h, o_proj_h, xt, dgu, down, proj, out, sem
):
    gate, up = pl.ds(0, N), pl.ds(N, N)
    moves = [
        (xt_h, xt),
        (dgu_h.at[:, gate], dgu.at[:, gate]),
        (dgu_h.at[:, up], dgu.at[:, up]),
        (down_h, down),
        (proj_h, proj),
        (out.at[:, gate], o_gate_h),
        (out.at[:, up], o_up_h),
        (down, o_down_h),
        (proj, o_proj_h),
    ]
    copies = [
        pltpu.make_async_copy(src, dst, sem.at[index]) for index, (src, dst) in enumerate(moves)
    ]
    for copy in copies[:5]:
        copy.start()
    copies[0].wait()
    for half, cols in enumerate((gate, up)):
        copies[1 + half].wait()
        out[:, cols] = dot(xt[...], dgu[:, cols]).astype(BF)
        copies[5 + half].start()
        copies[3 + half].wait()
        copies[7 + half].start()
    for copy in copies[5:]:
        copy.wait()


def per_device(
    teacher_in, teacher_gain, teacher_gate, teacher_up, teacher_down, align_layer,
    student_in, student_gain, student_gate, student_up, student_down, projection,
):
    any_space = pl.BlockSpec(memory_space=pl.ANY)
    v = pltpu.VMEM
    scratch = [
        v((T, KT), BF), v((1, KT), F32), v((2 * KT, W2), BF), v((2 * N, KT), BF), v((1, T), jnp.int32),
        v((T, KS), BF), v((1, KS), F32), v((KS, W2), BF), v((N, 4 * KS), BF), v((4 * KS, KT), BF),
        v((64, 4 * KS), BF),
        v((T, KS), BF), v((KS, T), BF), v((T, 2 * KT), BF), v((T, 128), F32), v((T, N), BF),
        v((T, WS), BF), v((4, 3, 16, WS), BF), v((3, 16, WS), BF), v((3, 16, WS), BF),
        v((T, N), BF), v((T, W2), BF),
        v((T, WS), BF), v((T // 2, WS), BF), v((T, WS), BF), v((7, 16, WS), BF),
        v((T, KT), BF), v((3, 64, KT), BF),
        v((64, 4 * KS), BF), v((15, 16, KS), BF), v((64, 4 * KS), BF),
        v((64, KT), BF), v((3, 16, KT), BF), v((T, KT), BF),
        v((64, 4 * KS), BF), v((15, 16, KS), BF), v((64, 4 * KS), BF),
        v((64, N), BF), v((3, 16, N), BF), v((T, N), BF), v((T, W2), BF),
        v((T, KS), BF), v((T, KS), BF),
        v((N, KS), BF), v((KS, KT), BF),
        pltpu.SemaphoreType.DMA((N_REMOTE,)),
        pltpu.SemaphoreType.DMA((N_REMOTE,)),
        pltpu.SemaphoreType.DMA((N_LOCAL,)),
    ]
    out = [
        jax.ShapeDtypeStruct((KS, T), BF),
        jax.ShapeDtypeStruct((T, W2), BF),
        jax.ShapeDtypeStruct((N, KS), BF),
        jax.ShapeDtypeStruct((KS, KT), BF),
    ]
    held = pl.pallas_call(
        kernel,
        name="distill",
        out_shape=out,
        in_specs=[any_space] * 12,
        out_specs=[any_space] * 4,
        scratch_shapes=scratch,
        cost_estimate=pl.CostEstimate(flops=3 * 10**9, bytes_accessed=10**7, transcendentals=10**5),
        compiler_params=pltpu.CompilerParams(
            collective_id=0, has_side_effects=True, vmem_limit_bytes=60 * 2**20
        ),
    )(
        teacher_in, teacher_gain.reshape(1, KT), teacher_gate, teacher_up,
        teacher_down.reshape(2 * N, KT), align_layer.reshape(1, T),
        student_in, student_gain.reshape(1, KS), student_gate, student_up, student_down, projection,
    )
    return pl.pallas_call(
        results,
        name="results",
        out_shape=[
            jax.ShapeDtypeStruct((KS, N), BF),
            jax.ShapeDtypeStruct((KS, N), BF),
            jax.ShapeDtypeStruct((N, KS), BF),
            jax.ShapeDtypeStruct((KS, KT), BF),
        ],
        in_specs=[any_space] * 4,
        out_specs=[any_space] * 4,
        scratch_shapes=[
            v((KS, T), BF), v((T, W2), BF), v((N, KS), BF), v((KS, KT), BF),
            v((KS, W2), BF), pltpu.SemaphoreType.DMA((9,)),
        ],
        cost_estimate=pl.CostEstimate(flops=3 * 10**8, bytes_accessed=4 * 10**6, transcendentals=0),
        compiler_params=pltpu.CompilerParams(vmem_limit_bytes=60 * 2**20),
    )(*held)


def solution(mesh):
    in_specs = (
        P(None, ("grp", "tp")),
        P(("grp", "tp")),
        P(None, ("grp", "tp"), "seq"),
        P(None, ("grp", "tp"), "seq"),
        P(None, "seq", ("grp", "tp")),
        P(),
        P(None, "seq"),
        P("seq"),
        P("seq", ("grp", "tp")),
        P("seq", ("grp", "tp")),
        P(("grp", "tp"), "seq"),
        P("seq", ("grp", "tp")),
    )
    out_specs = (
        P("seq", ("grp", "tp")),
        P("seq", ("grp", "tp")),
        P(("grp", "tp"), "seq"),
        P("seq", ("grp", "tp")),
    )
    return jax.shard_map(
        per_device, mesh=mesh, in_specs=in_specs, out_specs=out_specs, check_vma=False
    )
```

```python
import functools
import math

import jax
import jax.numpy as jnp
from jax import lax
from jax.experimental import pallas as pl
from jax.experimental.pallas import tpu as pltpu
from jax.sharding import PartitionSpec as P

MESH = pl.DeviceIdType.MESH
BF = jnp.bfloat16
F32 = jnp.float32

T = 256
DT = 8192
DS = 4096
KT = 512
KS = 256
N = 896
W2 = 2 * N
WS = W2 + 128

GOFF = [
    (a, b, c) for b in (1, 3, 2, 0) for a in (0, 1) for c in (0, 1) if (a, b, c) != (0, 0, 0)
]


def dot(a, b):
    return lax.dot_general(a, b, (((1,), (0,)), ((), ())), preferred_element_type=F32)


def dot_nt(a, b):
    return lax.dot_general(a, b, (((1,), (1,)), ((), ())), preferred_element_type=F32)


CHIPS = [o for o in GOFF if o[2] == 0]


class Sems:
    def __init__(self, send, recv):
        self.send, self.recv, self.started = send, recv, []

    def start(self, src, dst, device):
        index = len(self.started)
        copy = pltpu.make_async_remote_copy(
            src_ref=src,
            dst_ref=dst,
            send_sem=self.send.at[index],
            recv_sem=self.recv.at[index],
            device_id=device,
            device_id_type=MESH,
        )
        copy.start()
        self.started.append(copy)
        return copy


def squares(total):
    rows = total.shape[0]
    wide = jnp.broadcast_to(total, (rows, 128))
    high = wide.astype(BF)
    low = (wide - high.astype(F32)).astype(BF)
    lane = lax.broadcasted_iota(jnp.int32, (rows, 128), 1)
    return jnp.where(lane < 64, high.astype(F32), low.astype(F32)).astype(BF)


def total_of(columns):
    lane = lax.broadcasted_iota(jnp.int32, columns.shape, 1)
    picked = jnp.where((lane == 0) | (lane == 64), columns, 0.0)
    return jnp.sum(picked, axis=1, keepdims=True)


def kernel(
    t_in_h, t_gain_h, t_gate_h, t_up_h, t_down_h, align_h,
    s_in_h, s_gain_h, s_gate_h, s_up_h, s_down_h, proj_h,
    xt_h, dgu_h, o_down_h, o_proj_h,
    t_in, t_gain, t_w, t_down, align,
    s_in, s_gain, s_w, down, proj, s_tok,
    xg, xgt, xt, hm, h_t,
    pb, rfar, bsum, rby, zb, rbz, h_s, coef,
    pc, rcore, pcore, rc, tp, rt, pd, rd, state,
    pe, rez, dp, pf, rf, d_state,
    pg, rgz, dh, dgu, state_f, d_state_f,
    o_down, o_proj,
    send, recv, lsem,
):
    grp, seq, tpi = lax.axis_index("grp"), lax.axis_index("seq"), lax.axis_index("tp")
    zh, y = seq // 4, seq % 4
    x, core = tpi // 2, tpi % 2

    def s_dev(dz, dy):
        return (grp, ((zh + dz) % 4) * 4 + (y + dy) % 4, tpi)

    def g_dev(a, b, c):
        return ((grp + a) % 2, seq, ((x + b) % 4) * 2 + (core + c) % 2)

    def g_rows(a=0, b=0, c=0):
        owner = ((core + c) % 2) * 8 + ((grp + a) % 2) * 4 + (x + b) % 4
        return pl.ds(pl.multiple_of(owner * 16, 16), 16)

    def half_rows(c=0):
        return pl.ds(pl.multiple_of(((core + c) % 2) * 128, 128), 128)

    def g_block(a=0, b=0, c=0):
        row = ((core + c) % 2) * 2 + (grp + a) % 2
        return (
            pl.ds(pl.multiple_of(row * 16, 16), 16),
            pl.ds(pl.multiple_of(((x + b) % 4) * KS, KS), KS),
        )

    def s_rows(dz=0, dy=0):
        owner = ((y + dy) % 4) * 4 + (zh + dz) % 4
        return pl.ds(pl.multiple_of(owner * 16, 16), 16)

    def y_rows(dy=0):
        return pl.ds(pl.multiple_of(((y + dy) % 4) * 64, 64), 64)

    def y_half(dy, half):
        return pl.ds(pl.multiple_of(((y + dy) % 4) * 64 + half * 32, 32), 32)

    def z_rows(dz=0):
        return pl.ds(pl.multiple_of(((zh + dz) % 4) * 16, 16), 16)

    def feat(dy=0, start=0, count=KS):
        return pl.ds(pl.multiple_of(((y + dy) % 4) * KS + start, 128), count)

    sems = Sems(send, recv)
    loads = []

    def load(src, dst):
        copy = pltpu.make_async_copy(src, dst, lsem.at[len(loads)])
        copy.start()
        loads.append(copy)
        return copy

    def arrived(copies):
        for copy in copies:
            copy.wait_recv()

    l_sd = load(s_down_h, down.at[y])
    l_s = [
        load(s_in_h, s_in),
        load(s_gain_h, s_gain),
        load(s_gate_h, s_w.at[:, pl.ds(0, N)]),
        load(s_up_h, s_w.at[:, pl.ds(N, N)]),
    ]
    barrier = pltpu.get_barrier_semaphore()
    partners = [s_dev(0, k) for k in (1, 2, 3)] + [s_dev(k, 0) for k in (1, 2, 3)]
    partners += [g_dev(*o) for o in GOFF]
    for device in partners:
        pl.semaphore_signal(barrier, inc=1, device_id=device, device_id_type=MESH)

    def y_sum(src, slots, dz, columns):
        total = src[s_rows(dz), columns].astype(F32)
        for index in range(2):
            total = total + slots[index, z_rows(dz), columns].astype(F32)
        return total

    def rs_z(src, slots):
        return [
            sems.start(src.at[z_rows(dz)], slots.at[dz - 1], s_dev(dz, 0)) for dz in (2, 1, 3)
        ]

    def z_total(src, slots):
        total = src[z_rows(), :].astype(F32)
        for index in range(3):
            total = total + slots[index].astype(F32)
        return total

    def ag_z(buf):
        return [sems.start(buf.at[s_rows()], buf.at[s_rows()], s_dev(dz, 0)) for dz in (2, 1, 3)]

    def to_y(src, dst):
        return [sems.start(src(dy), dst(dy), s_dev(0, dy)) for dy in (2, 1, 3)]

    def rs_g(src, slots):
        return [
            sems.start(src.at[g_block(*o)], slots.at[i], g_dev(*o)) for i, o in enumerate(GOFF)
        ]

    def ag_g(buf):
        return [sems.start(buf.at[g_block()], buf.at[g_block()], g_dev(*o)) for o in GOFF]

    def g_total(src, slots):
        total = src[g_block()].astype(F32)
        for index in range(15):
            total = total + slots[index].astype(F32)
        return total

    def neighbours(src, dst):
        return [sems.start(src, dst, s_dev(0, dy)) for dy in (1, 3)]

    def proj_half(dy, half):
        return proj.at[feat(dy, half * 128, 128), :]

    def down_half(dy, half):
        return down.at[(y + dy) % 4, pl.ds(half * (N // 2), N // 2), :]

    def ag_y(buf):
        return neighbours(buf.at[y_rows()], buf.at[y_rows()])

    def relay_rows(copies, buf):
        return relay(copies, lambda dy, half: buf.at[y_half(dy, half)])

    def relay(copies, part):
        arrived(copies)
        return [
            sems.start(part(3, 0), part(3, 0), s_dev(0, 1)),
            sems.start(part(1, 1), part(1, 1), s_dev(0, 3)),
        ]


    for copy in l_s[:2]:
        copy.wait()
    wide = s_in[...].astype(F32)
    xg[...] = (wide * s_gain[...]).astype(BF)
    pb[:, W2:] = squares(jnp.sum(wide * wide, axis=1, keepdims=True))
    for copy in l_s[2:]:
        copy.wait()
    l_t = [load(t_in_h, t_in), load(t_gain_h, t_gain), load(align_h, align)]
    for layer in range(2):
        rows = pl.ds(layer * KT, KT)
        l_t.append(load(t_gate_h.at[layer], t_w.at[rows, pl.ds(0, N)]))
        l_t.append(load(t_up_h.at[layer], t_w.at[rows, pl.ds(N, N)]))
    l_p = load(proj_h, proj.at[feat(), :])
    l_td = load(t_down_h, t_down)
    for tile in range(7):
        cols = pl.ds(tile * 256, 256)
        pb[:, cols] = dot(xg[...], s_w[:, cols]).astype(BF)

    pl.semaphore_wait(barrier, len(partners))
    b_far = [
        sems.start(pb.at[y_half(2, 0)], rfar.at[0], s_dev(0, 1)),
        sems.start(pb.at[y_half(2, 1)], rfar.at[1], s_dev(0, 3)),
    ]
    l_sd.wait()
    w_down = neighbours(down.at[y], down.at[y])
    b_y = [
        sems.start(pb.at[y_half(1, 1)], rby.at[0, pl.ds(32, 32)], s_dev(0, 1)),
        sems.start(pb.at[y_half(3, 0)], rby.at[1, pl.ds(0, 32)], s_dev(0, 3)),
    ]

    for copy in l_t:
        copy.wait()
    diagonal = lax.broadcasted_iota(jnp.int32, (T, T), 0) == lax.broadcasted_iota(
        jnp.int32, (T, T), 1
    )
    layer_of = jnp.sum(
        jnp.where(diagonal, jnp.broadcast_to(align[...].astype(F32), (T, T)), 0.0),
        axis=1,
        keepdims=True,
    )
    hm[...] = jnp.broadcast_to(layer_of, (T, 128))
    wide = t_in[...].astype(F32)
    scaled = wide * t_gain[...]
    xt[:, :KT] = jnp.where(layer_of < 0.5, scaled, 0.0).astype(BF)
    xt[:, KT:] = jnp.where(layer_of < 0.5, 0.0, scaled).astype(BF)
    pc[:, W2:] = squares(jnp.sum(wide * wide, axis=1, keepdims=True))

    for tile in range(7):
        cols = pl.ds(tile * 256, 256)
        pc[:, cols] = dot(xt[...], t_w[:, cols]).astype(BF)

    c_core = sems.start(pc.at[half_rows(1)], rcore, g_dev(0, 0, 1))
    xgt[...] = xg[...].T
    for half, dy in ((0, 1), (1, 3)):
        arrived([b_far[half]])
        rows = y_half(dy, half)
        both = pb[rows, :W2].astype(F32) + rfar[half, :, :W2].astype(F32)
        bsum[half, :, :W2] = both.astype(BF)
        both = total_of(pb[rows, W2:].astype(F32) + rfar[half, :, W2:].astype(F32))
        bsum[half, :, W2:] = squares(both)
        slot = rby.at[half, pl.ds(half * 32, 32)]
        b_y.append(sems.start(bsum.at[half], slot, s_dev(0, dy)))
    w_down += relay(w_down, down_half)
    l_p.wait()
    arrived([c_core])
    pair = pc[half_rows(), :W2].astype(F32) + rcore[:, :W2].astype(F32)
    pcore[half_rows(), :W2] = pair.astype(BF)
    pair = total_of(pc[half_rows(), W2:].astype(F32) + rcore[:, W2:].astype(F32))
    pcore[half_rows(), W2:] = squares(pair)
    c_rs = [sems.start(pcore.at[g_rows(*o)], rc.at[i], g_dev(*o)) for i, o in enumerate(CHIPS)]

    def c_total(columns):
        total = pcore[g_rows(), columns].astype(F32)
        for index in range(7):
            total = total + rc[index, :, columns].astype(F32)
        return total

    b_z = []
    arrived(b_y)
    for dz in (2, 1, 3):
        zb[dz - 1, :, :W2] = y_sum(pb, rby, dz, pl.ds(0, W2)).astype(BF)
        zb[dz - 1, :, W2:] = squares(total_of(y_sum(pb, rby, dz, pl.ds(W2, 128))))
        b_z.append(sems.start(zb.at[dz - 1], rbz.at[dz - 1], s_dev(dz, 0)))
    w_proj = neighbours(proj.at[feat(), :], proj.at[feat(), :])
    w_tok = to_y(lambda dy: s_in.at[y_rows(dy)], lambda dy: s_tok.at[:, feat()])
    s_tok[:, feat()] = s_in[y_rows(), :]

    def b_total(columns):
        total = y_sum(pb, rby, 0, columns)
        for index in range(3):
            total = total + rbz[index, :, columns].astype(F32)
        return total

    arrived(b_z)
    scale = lax.rsqrt(total_of(b_total(pl.ds(W2, 128))) / DS + 1e-05)
    g = b_total(pl.ds(0, N)) * scale
    u = b_total(pl.ds(N, N)) * scale
    q = jax.nn.sigmoid(g)
    h_s[s_rows(), :] = (g * q * u).astype(BF)
    b_ag = ag_z(h_s)
    coef[s_rows(), :N] = (scale * u * q * (1.0 + g * (1.0 - q))).astype(BF)
    coef[s_rows(), N:] = (scale * g * q).astype(BF)

    arrived(c_rs)
    scale = lax.rsqrt(total_of(c_total(pl.ds(W2, 128))) / DT + 1e-05)
    g = c_total(pl.ds(0, N)) * scale
    u = c_total(pl.ds(N, N)) * scale
    h_t[g_rows(), :] = (g * jax.nn.sigmoid(g) * u).astype(BF)
    c_ag = [sems.start(h_t.at[g_rows()], h_t.at[g_rows()], g_dev(*o)) for o in CHIPS]

    arrived(b_ag)
    arrived(w_down[2:])

    for tile in range(4):
        cols = pl.ds(tile * 256, 256)
        pd[:, cols] = dot(h_s[y_rows(), :], down[tile]).astype(BF)
    d_rs = rs_g(pd, rd)

    arrived(c_ag)
    c_core = sems.start(h_t.at[half_rows()], h_t.at[half_rows()], g_dev(0, 0, 1))
    w_proj += relay(w_proj, proj_half)
    l_td.wait()
    arrived([c_core])
    first = hm[:, 0:1] < 0.5
    zero = jnp.zeros((), BF)
    for half in range(2):
        cols = pl.ds(half * 256, 256)
        tp[:, cols] = (
            dot(jnp.where(first, h_t[...], zero), t_down[:N, cols])
            + dot(jnp.where(first, zero, h_t[...]), t_down[N:, cols])
        ).astype(BF)
    t_rs = to_y(lambda dy: tp.at[y_rows(dy)], lambda dy: rt.at[dy - 1])

    arrived(w_tok)
    arrived(d_rs)
    state[g_block()] = (s_tok[g_block()].astype(F32) + g_total(pd, rd)).astype(BF)
    d_ag = ag_g(state)
    k_ag = ag_z(coef)
    h_ag = ag_y(h_s)
    arrived(w_proj[2:])
    arrived(t_rs)
    arrived(d_ag)

    for half in range(2):
        cols = pl.ds(half * 256, 256)
        target = tp[y_rows(), cols].astype(F32)
        for index in range(3):
            target = target + rt[index, :, cols].astype(F32)
        pe[:, cols] = (dot(state[...], proj[:, cols]) - target).astype(BF)
    e_z = rs_z(pe, rez)
    s_aa = to_y(lambda dy: state.at[:, feat(dy)], lambda dy: state_f.at[y_rows()])
    state_f[y_rows(), :] = state[:, feat()]
    h_ag += relay_rows(h_ag, h_s)
    arrived(e_z)
    dp[s_rows(), :] = (
        (z_total(pe, rez) - t_in[s_rows(), :].astype(F32)) * (1.0 / math.sqrt(T))
    ).astype(BF)
    e_ag = ag_z(dp)
    arrived(k_ag)
    k_ay = ag_y(coef)
    arrived(e_ag)

    for tile in range(4):
        cols = pl.ds(tile * 256, 256)
        pf[:, cols] = dot_nt(dp[y_rows(), :], proj[cols, :]).astype(BF)
    f_rs = rs_g(pf, rf)
    p_ag = ag_y(dp)
    arrived(f_rs)
    d_state[g_block()] = g_total(pf, rf).astype(BF)
    f_ag = ag_g(d_state)
    k_ay += relay_rows(k_ay, coef)
    stores = []

    def store(src, dst):
        copy = pltpu.make_async_copy(src, dst, lsem.at[len(loads) + len(stores)])
        copy.start()
        stores.append(copy)

    store(xgt, xt_h)
    arrived(s_aa)
    state_t = state_f[...].T
    arrived(f_ag)

    d_hidden = dot_nt(d_state[:, :KS], down[0])
    for tile in range(1, 4):
        d_hidden += dot_nt(d_state[:, tile * KS : (tile + 1) * KS], down[tile])
    pg[...] = d_hidden.astype(BF)
    g_z = rs_z(pg, rgz)
    d_aa = to_y(lambda dy: d_state.at[:, feat(dy)], lambda dy: d_state_f.at[y_rows()])
    d_state_f[y_rows(), :] = d_state[:, feat()]
    p_ag += relay_rows(p_ag, dp)
    arrived(p_ag[2:])
    o_proj[...] = dot(state_t, dp[...]).astype(BF)
    store(o_proj, o_proj_h)
    arrived(g_z)
    dh[s_rows(), :] = z_total(pg, rgz).astype(BF)
    g_az = {dz: sems.start(dh.at[s_rows()], dh.at[s_rows()], s_dev(dz, 0)) for dz in (2, 1, 3)}
    g_ay = [sems.start(dh.at[s_rows()], dh.at[s_rows()], s_dev(0, dy)) for dy in (2, 1, 3)]
    arrived(h_ag[2:])
    arrived(d_aa)
    o_down[...] = dot(h_s[...].T, d_state_f[...]).astype(BF)
    store(o_down, o_down_h)
    for dz in (1, 3, 2):
        arrived([g_az[dz]])
        rows = s_rows(4 - dz)
        g_ay += [sems.start(dh.at[rows], dh.at[rows], s_dev(0, dy)) for dy in (2, 1, 3)]
    arrived(k_ay[2:])
    arrived(g_ay)
    for half in range(2):
        cols = pl.ds(half * N, N)
        dgu[:, cols] = (dh[...].astype(F32) * coef[:, cols].astype(F32)).astype(BF)
        store(dgu.at[:, cols], dgu_h.at[:, cols])

    for copy in sems.started:
        copy.wait_send()
    for copy in stores:
        copy.wait()


N_REMOTE = 160
N_LOCAL = 14 + 5


def results(
    xt_h, dgu_h, down_h, proj_h, o_gate_h, o_up_h, o_down_h, o_proj_h, xt, dgu, down, proj, out, sem
):
    gate, up = pl.ds(0, N), pl.ds(N, N)
    moves = [
        (xt_h, xt),
        (dgu_h.at[:, gate], dgu.at[:, gate]),
        (dgu_h.at[:, up], dgu.at[:, up]),
        (down_h, down),
        (proj_h, proj),
        (out.at[:, gate], o_gate_h),
        (out.at[:, up], o_up_h),
        (down, o_down_h),
        (proj, o_proj_h),
    ]
    copies = [
        pltpu.make_async_copy(src, dst, sem.at[index]) for index, (src, dst) in enumerate(moves)
    ]
    for copy in copies[:5]:
        copy.start()
    copies[0].wait()
    for half, cols in enumerate((gate, up)):
        copies[1 + half].wait()
        out[:, cols] = dot(xt[...], dgu[:, cols]).astype(BF)
        copies[5 + half].start()
        copies[3 + half].wait()
        copies[7 + half].start()
    for copy in copies[5:]:
        copy.wait()


def per_device(
    teacher_in, teacher_gain, teacher_gate, teacher_up, teacher_down, align_layer,
    student_in, student_gain, student_gate, student_up, student_down, projection,
):
    any_space = pl.BlockSpec(memory_space=pl.ANY)
    v = pltpu.VMEM
    scratch = [
        v((T, KT), BF), v((1, KT), F32), v((2 * KT, W2), BF), v((2 * N, KT), BF), v((1, T), jnp.int32),
        v((T, KS), BF), v((1, KS), F32), v((KS, W2), BF), v((4, N, KS), BF), v((4 * KS, KT), BF),
        v((64, 4 * KS), BF),
        v((T, KS), BF), v((KS, T), BF), v((T, 2 * KT), BF), v((T, 128), F32), v((T, N), BF),
        v((T, WS), BF), v((2, 32, WS), BF), v((2, 32, WS), BF), v((2, 64, WS), BF),
        v((3, 16, WS), BF), v((3, 16, WS), BF),
        v((T, N), BF), v((T, W2), BF),
        v((T, WS), BF), v((T // 2, WS), BF), v((T, WS), BF), v((7, 16, WS), BF),
        v((T, KT), BF), v((3, 64, KT), BF),
        v((64, 4 * KS), BF), v((15, 16, KS), BF), v((64, 4 * KS), BF),
        v((64, KT), BF), v((3, 16, KT), BF), v((T, KT), BF),
        v((64, 4 * KS), BF), v((15, 16, KS), BF), v((64, 4 * KS), BF),
        v((64, N), BF), v((3, 16, N), BF), v((T, N), BF), v((T, W2), BF),
        v((T, KS), BF), v((T, KS), BF),
        v((N, KS), BF), v((KS, KT), BF),
        pltpu.SemaphoreType.DMA((N_REMOTE,)),
        pltpu.SemaphoreType.DMA((N_REMOTE,)),
        pltpu.SemaphoreType.DMA((N_LOCAL,)),
    ]
    out = [
        jax.ShapeDtypeStruct((KS, T), BF),
        jax.ShapeDtypeStruct((T, W2), BF),
        jax.ShapeDtypeStruct((N, KS), BF),
        jax.ShapeDtypeStruct((KS, KT), BF),
    ]
    held = pl.pallas_call(
        kernel,
        name="distill",
        out_shape=out,
        in_specs=[any_space] * 12,
        out_specs=[any_space] * 4,
        scratch_shapes=scratch,
        cost_estimate=pl.CostEstimate(flops=3 * 10**9, bytes_accessed=10**7, transcendentals=10**5),
        compiler_params=pltpu.CompilerParams(
            collective_id=0, has_side_effects=True, vmem_limit_bytes=60 * 2**20
        ),
    )(
        teacher_in, teacher_gain.reshape(1, KT), teacher_gate, teacher_up,
        teacher_down.reshape(2 * N, KT), align_layer.reshape(1, T),
        student_in, student_gain.reshape(1, KS), student_gate, student_up, student_down, projection,
    )
    return pl.pallas_call(
        results,
        name="results",
        out_shape=[
            jax.ShapeDtypeStruct((KS, N), BF),
            jax.ShapeDtypeStruct((KS, N), BF),
            jax.ShapeDtypeStruct((N, KS), BF),
            jax.ShapeDtypeStruct((KS, KT), BF),
        ],
        in_specs=[any_space] * 4,
        out_specs=[any_space] * 4,
        scratch_shapes=[
            v((KS, T), BF), v((T, W2), BF), v((N, KS), BF), v((KS, KT), BF),
            v((KS, W2), BF), pltpu.SemaphoreType.DMA((9,)),
        ],
        cost_estimate=pl.CostEstimate(flops=3 * 10**8, bytes_accessed=4 * 10**6, transcendentals=0),
        compiler_params=pltpu.CompilerParams(vmem_limit_bytes=60 * 2**20),
    )(*held)


def solution(mesh):
    in_specs = (
        P(None, ("grp", "tp")),
        P(("grp", "tp")),
        P(None, ("grp", "tp"), "seq"),
        P(None, ("grp", "tp"), "seq"),
        P(None, "seq", ("grp", "tp")),
        P(),
        P(None, "seq"),
        P("seq"),
        P("seq", ("grp", "tp")),
        P("seq", ("grp", "tp")),
        P(("grp", "tp"), "seq"),
        P("seq", ("grp", "tp")),
    )
    out_specs = (
        P("seq", ("grp", "tp")),
        P("seq", ("grp", "tp")),
        P(("grp", "tp"), "seq"),
        P("seq", ("grp", "tp")),
    )
    return jax.shard_map(
        per_device, mesh=mesh, in_specs=in_specs, out_specs=out_specs, check_vma=False
    )
```

```python
import functools
import math

import jax
import jax.numpy as jnp
from jax import lax
from jax.experimental import pallas as pl
from jax.experimental.pallas import tpu as pltpu
from jax.sharding import PartitionSpec as P

MESH = pl.DeviceIdType.MESH
BF = jnp.bfloat16
F32 = jnp.float32

T = 256
DT = 8192
DS = 4096
KT = 512
KS = 256
N = 896
W2 = 2 * N
WS = W2 + 128

GOFF = [
    (a, b, c) for b in (1, 3, 2, 0) for a in (0, 1) for c in (0, 1) if (a, b, c) != (0, 0, 0)
]


def dot(a, b):
    return lax.dot_general(a, b, (((1,), (0,)), ((), ())), preferred_element_type=F32)


def dot_nt(a, b):
    return lax.dot_general(a, b, (((1,), (1,)), ((), ())), preferred_element_type=F32)


CHIPS = [o for o in GOFF if o[2] == 0]


class Sems:
    def __init__(self, send, recv):
        self.send, self.recv, self.started = send, recv, []

    def start(self, src, dst, device):
        index = len(self.started)
        copy = pltpu.make_async_remote_copy(
            src_ref=src,
            dst_ref=dst,
            send_sem=self.send.at[index],
            recv_sem=self.recv.at[index],
            device_id=device,
            device_id_type=MESH,
        )
        copy.start()
        self.started.append(copy)
        return copy


def squares(total):
    rows = total.shape[0]
    wide = jnp.broadcast_to(total, (rows, 128))
    high = wide.astype(BF)
    low = (wide - high.astype(F32)).astype(BF)
    lane = lax.broadcasted_iota(jnp.int32, (rows, 128), 1)
    return jnp.where(lane < 64, high.astype(F32), low.astype(F32)).astype(BF)


def total_of(columns):
    lane = lax.broadcasted_iota(jnp.int32, columns.shape, 1)
    picked = jnp.where((lane == 0) | (lane == 64), columns, 0.0)
    return jnp.sum(picked, axis=1, keepdims=True)


def kernel(
    t_in_h, t_gain_h, t_gate_h, t_up_h, t_down_h, align_h,
    s_in_h, s_gain_h, s_gate_h, s_up_h, s_down_h, proj_h,
    xt_h, dgu_h, o_down_h, o_proj_h,
    t_in, t_gain, t_w, t_down, align,
    s_in, s_gain, s_w, down, proj, s_tok,
    xg, xgt, xt, hm, h_t,
    pb, rfar, bsum, rby, zb, rbz, h_s, coef,
    pc, rcore, pcore, rc, tp, rt, pd, rd, state,
    pe, rez, dp, pf, rf, d_state,
    pg, rgz, dh, dgu, state_f, d_state_f,
    o_down, o_proj,
    send, recv, lsem,
):
    grp, seq, tpi = lax.axis_index("grp"), lax.axis_index("seq"), lax.axis_index("tp")
    zh, y = seq // 4, seq % 4
    x, core = tpi // 2, tpi % 2

    def s_dev(dz, dy):
        return (grp, ((zh + dz) % 4) * 4 + (y + dy) % 4, tpi)

    def g_dev(a, b, c):
        return ((grp + a) % 2, seq, ((x + b) % 4) * 2 + (core + c) % 2)

    def g_rows(a=0, b=0, c=0):
        owner = ((core + c) % 2) * 8 + ((grp + a) % 2) * 4 + (x + b) % 4
        return pl.ds(pl.multiple_of(owner * 16, 16), 16)

    def half_rows(c=0):
        return pl.ds(pl.multiple_of(((core + c) % 2) * 128, 128), 128)

    def g_block(a=0, b=0, c=0):
        row = ((core + c) % 2) * 2 + (grp + a) % 2
        return (
            pl.ds(pl.multiple_of(row * 16, 16), 16),
            pl.ds(pl.multiple_of(((x + b) % 4) * KS, KS), KS),
        )

    def s_rows(dz=0, dy=0):
        owner = ((y + dy) % 4) * 4 + (zh + dz) % 4
        return pl.ds(pl.multiple_of(owner * 16, 16), 16)

    def y_rows(dy=0):
        return pl.ds(pl.multiple_of(((y + dy) % 4) * 64, 64), 64)

    def y_half(dy, half):
        return pl.ds(pl.multiple_of(((y + dy) % 4) * 64 + half * 32, 32), 32)

    def z_rows(dz=0):
        return pl.ds(pl.multiple_of(((zh + dz) % 4) * 16, 16), 16)

    def feat(dy=0, start=0, count=KS):
        return pl.ds(pl.multiple_of(((y + dy) % 4) * KS + start, 128), count)

    sems = Sems(send, recv)
    loads = []

    def load(src, dst):
        copy = pltpu.make_async_copy(src, dst, lsem.at[len(loads)])
        copy.start()
        loads.append(copy)
        return copy

    def arrived(copies):
        for copy in copies:
            copy.wait_recv()

    l_sd = load(s_down_h, down.at[y])
    l_s = [
        load(s_in_h, s_in),
        load(s_gain_h, s_gain),
        load(s_gate_h, s_w.at[:, pl.ds(0, N)]),
        load(s_up_h, s_w.at[:, pl.ds(N, N)]),
    ]
    barrier = pltpu.get_barrier_semaphore()
    partners = [s_dev(0, k) for k in (1, 2, 3)] + [s_dev(k, 0) for k in (1, 2, 3)]
    partners += [g_dev(*o) for o in GOFF]
    for device in partners:
        pl.semaphore_signal(barrier, inc=1, device_id=device, device_id_type=MESH)

    def y_sum(src, slots, dz, columns):
        total = src[s_rows(dz), columns].astype(F32)
        for index in range(2):
            total = total + slots[index, z_rows(dz), columns].astype(F32)
        return total

    def rs_z(src, slots):
        return [
            sems.start(src.at[z_rows(dz)], slots.at[dz - 1], s_dev(dz, 0)) for dz in (2, 1, 3)
        ]

    def z_total(src, slots):
        total = src[z_rows(), :].astype(F32)
        for index in range(3):
            total = total + slots[index].astype(F32)
        return total

    def ag_z(buf):
        return [sems.start(buf.at[s_rows()], buf.at[s_rows()], s_dev(dz, 0)) for dz in (2, 1, 3)]

    def to_y(src, dst):
        return [sems.start(src(dy), dst(dy), s_dev(0, dy)) for dy in (2, 1, 3)]

    def rs_g(src, slots):
        return [
            sems.start(src.at[g_block(*o)], slots.at[i], g_dev(*o)) for i, o in enumerate(GOFF)
        ]

    def ag_g(buf):
        return [sems.start(buf.at[g_block()], buf.at[g_block()], g_dev(*o)) for o in GOFF]

    def g_total(src, slots):
        total = src[g_block()].astype(F32)
        for index in range(15):
            total = total + slots[index].astype(F32)
        return total

    def neighbours(src, dst):
        return [sems.start(src, dst, s_dev(0, dy)) for dy in (1, 3)]

    def proj_half(dy, half):
        return proj.at[feat(dy, half * 128, 128), :]

    def down_half(dy, half):
        return down.at[(y + dy) % 4, pl.ds(half * (N // 2), N // 2), :]

    def ag_y(buf):
        return neighbours(buf.at[y_rows()], buf.at[y_rows()])

    def relay_rows(copies, buf):
        return relay(copies, lambda dy, half: buf.at[y_half(dy, half)])

    def half_to(part, on):
        return [
            sems.start(part(0, 1 - on), part(0, 1 - on), s_dev(0, 1)),
            sems.start(part(0, on), part(0, on), s_dev(0, 3)),
        ]

    def relay(copies, part):
        arrived(copies)
        return [
            sems.start(part(3, 0), part(3, 0), s_dev(0, 1)),
            sems.start(part(1, 1), part(1, 1), s_dev(0, 3)),
        ]


    for copy in l_s[:2]:
        copy.wait()
    wide = s_in[...].astype(F32)
    xg[...] = (wide * s_gain[...]).astype(BF)
    pb[:, W2:] = squares(jnp.sum(wide * wide, axis=1, keepdims=True))
    for copy in l_s[2:]:
        copy.wait()
    l_t = [load(t_in_h, t_in), load(t_gain_h, t_gain), load(align_h, align)]
    for layer in range(2):
        rows = pl.ds(layer * KT, KT)
        l_t.append(load(t_gate_h.at[layer], t_w.at[rows, pl.ds(0, N)]))
        l_t.append(load(t_up_h.at[layer], t_w.at[rows, pl.ds(N, N)]))
    l_p = load(proj_h, proj.at[feat(), :])
    l_td = load(t_down_h, t_down)
    for tile in range(7):
        cols = pl.ds(tile * 256, 256)
        pb[:, cols] = dot(xg[...], s_w[:, cols]).astype(BF)

    pl.semaphore_wait(barrier, len(partners))
    b_far = [
        sems.start(pb.at[y_half(2, 0)], rfar.at[0], s_dev(0, 1)),
        sems.start(pb.at[y_half(2, 1)], rfar.at[1], s_dev(0, 3)),
    ]
    l_sd.wait()
    w_down = half_to(down_half, 1)
    b_y = [
        sems.start(pb.at[y_half(1, 1)], rby.at[0, pl.ds(32, 32)], s_dev(0, 1)),
        sems.start(pb.at[y_half(3, 0)], rby.at[1, pl.ds(0, 32)], s_dev(0, 3)),
    ]

    for copy in l_t:
        copy.wait()
    diagonal = lax.broadcasted_iota(jnp.int32, (T, T), 0) == lax.broadcasted_iota(
        jnp.int32, (T, T), 1
    )
    layer_of = jnp.sum(
        jnp.where(diagonal, jnp.broadcast_to(align[...].astype(F32), (T, T)), 0.0),
        axis=1,
        keepdims=True,
    )
    hm[...] = jnp.broadcast_to(layer_of, (T, 128))
    wide = t_in[...].astype(F32)
    scaled = wide * t_gain[...]
    xt[:, :KT] = jnp.where(layer_of < 0.5, scaled, 0.0).astype(BF)
    xt[:, KT:] = jnp.where(layer_of < 0.5, 0.0, scaled).astype(BF)
    pc[:, W2:] = squares(jnp.sum(wide * wide, axis=1, keepdims=True))

    for tile in range(7):
        cols = pl.ds(tile * 256, 256)
        pc[:, cols] = dot(xt[...], t_w[:, cols]).astype(BF)

    c_core = sems.start(pc.at[half_rows(1)], rcore, g_dev(0, 0, 1))
    xgt[...] = xg[...].T
    for half, dy in ((0, 1), (1, 3)):
        arrived([b_far[half]])
        rows = y_half(dy, half)
        both = pb[rows, :W2].astype(F32) + rfar[half, :, :W2].astype(F32)
        bsum[half, :, :W2] = both.astype(BF)
        both = total_of(pb[rows, W2:].astype(F32) + rfar[half, :, W2:].astype(F32))
        bsum[half, :, W2:] = squares(both)
        slot = rby.at[half, pl.ds(half * 32, 32)]
        b_y.append(sems.start(bsum.at[half], slot, s_dev(0, dy)))
    w_down += relay(w_down, down_half)
    l_p.wait()
    arrived([c_core])
    pair = pc[half_rows(), :W2].astype(F32) + rcore[:, :W2].astype(F32)
    pcore[half_rows(), :W2] = pair.astype(BF)
    pair = total_of(pc[half_rows(), W2:].astype(F32) + rcore[:, W2:].astype(F32))
    pcore[half_rows(), W2:] = squares(pair)
    w_down += half_to(down_half, 0)
    c_rs = [sems.start(pcore.at[g_rows(*o)], rc.at[i], g_dev(*o)) for i, o in enumerate(CHIPS)]

    def c_total(columns):
        total = pcore[g_rows(), columns].astype(F32)
        for index in range(7):
            total = total + rc[index, :, columns].astype(F32)
        return total

    b_z = []
    arrived(b_y)
    for dz in (2, 1, 3):
        zb[dz - 1, :, :W2] = y_sum(pb, rby, dz, pl.ds(0, W2)).astype(BF)
        zb[dz - 1, :, W2:] = squares(total_of(y_sum(pb, rby, dz, pl.ds(W2, 128))))
        b_z.append(sems.start(zb.at[dz - 1], rbz.at[dz - 1], s_dev(dz, 0)))
    w_proj = neighbours(proj.at[feat(), :], proj.at[feat(), :])
    w_tok = to_y(lambda dy: s_in.at[y_rows(dy)], lambda dy: s_tok.at[:, feat()])
    s_tok[:, feat()] = s_in[y_rows(), :]

    def b_total(columns):
        total = y_sum(pb, rby, 0, columns)
        for index in range(3):
            total = total + rbz[index, :, columns].astype(F32)
        return total

    arrived(b_z)
    scale = lax.rsqrt(total_of(b_total(pl.ds(W2, 128))) / DS + 1e-05)
    g = b_total(pl.ds(0, N)) * scale
    u = b_total(pl.ds(N, N)) * scale
    q = jax.nn.sigmoid(g)
    h_s[s_rows(), :] = (g * q * u).astype(BF)
    b_ag = ag_z(h_s)
    coef[s_rows(), :N] = (scale * u * q * (1.0 + g * (1.0 - q))).astype(BF)
    coef[s_rows(), N:] = (scale * g * q).astype(BF)

    arrived(c_rs)
    scale = lax.rsqrt(total_of(c_total(pl.ds(W2, 128))) / DT + 1e-05)
    g = c_total(pl.ds(0, N)) * scale
    u = c_total(pl.ds(N, N)) * scale
    h_t[g_rows(), :] = (g * jax.nn.sigmoid(g) * u).astype(BF)
    c_ag = [sems.start(h_t.at[g_rows()], h_t.at[g_rows()], g_dev(*o)) for o in CHIPS]

    arrived(b_ag)
    arrived(w_down[2:])

    for tile in range(4):
        cols = pl.ds(tile * 256, 256)
        pd[:, cols] = dot(h_s[y_rows(), :], down[tile]).astype(BF)
    d_rs = rs_g(pd, rd)

    arrived(c_ag)
    c_core = sems.start(h_t.at[half_rows()], h_t.at[half_rows()], g_dev(0, 0, 1))
    w_proj += relay(w_proj, proj_half)
    l_td.wait()
    arrived([c_core])
    first = hm[:, 0:1] < 0.5
    zero = jnp.zeros((), BF)
    for half in range(2):
        cols = pl.ds(half * 256, 256)
        tp[:, cols] = (
            dot(jnp.where(first, h_t[...], zero), t_down[:N, cols])
            + dot(jnp.where(first, zero, h_t[...]), t_down[N:, cols])
        ).astype(BF)
    t_rs = to_y(lambda dy: tp.at[y_rows(dy)], lambda dy: rt.at[dy - 1])

    arrived(w_tok)
    arrived(d_rs)
    state[g_block()] = (s_tok[g_block()].astype(F32) + g_total(pd, rd)).astype(BF)
    d_ag = ag_g(state)
    k_ag = ag_z(coef)
    h_ag = ag_y(h_s)
    arrived(w_proj[2:])
    arrived(t_rs)
    arrived(d_ag)

    for half in range(2):
        cols = pl.ds(half * 256, 256)
        target = tp[y_rows(), cols].astype(F32)
        for index in range(3):
            target = target + rt[index, :, cols].astype(F32)
        pe[:, cols] = (dot(state[...], proj[:, cols]) - target).astype(BF)
    e_z = rs_z(pe, rez)
    s_aa = to_y(lambda dy: state.at[:, feat(dy)], lambda dy: state_f.at[y_rows()])
    state_f[y_rows(), :] = state[:, feat()]
    h_ag += relay_rows(h_ag, h_s)
    arrived(e_z)
    dp[s_rows(), :] = (
        (z_total(pe, rez) - t_in[s_rows(), :].astype(F32)) * (1.0 / math.sqrt(T))
    ).astype(BF)
    e_ag = ag_z(dp)
    arrived(k_ag)
    k_ay = ag_y(coef)
    arrived(e_ag)

    for tile in range(4):
        cols = pl.ds(tile * 256, 256)
        pf[:, cols] = dot_nt(dp[y_rows(), :], proj[cols, :]).astype(BF)
    f_rs = rs_g(pf, rf)
    p_ag = ag_y(dp)
    arrived(f_rs)
    d_state[g_block()] = g_total(pf, rf).astype(BF)
    f_ag = ag_g(d_state)
    k_ay += relay_rows(k_ay, coef)
    stores = []

    def store(src, dst):
        copy = pltpu.make_async_copy(src, dst, lsem.at[len(loads) + len(stores)])
        copy.start()
        stores.append(copy)

    store(xgt, xt_h)
    arrived(s_aa)
    state_t = state_f[...].T
    arrived(f_ag)

    d_hidden = dot_nt(d_state[:, :KS], down[0])
    for tile in range(1, 4):
        d_hidden += dot_nt(d_state[:, tile * KS : (tile + 1) * KS], down[tile])
    pg[...] = d_hidden.astype(BF)
    g_z = rs_z(pg, rgz)
    d_aa = to_y(lambda dy: d_state.at[:, feat(dy)], lambda dy: d_state_f.at[y_rows()])
    d_state_f[y_rows(), :] = d_state[:, feat()]
    p_ag += relay_rows(p_ag, dp)
    arrived(p_ag[2:])
    o_proj[...] = dot(state_t, dp[...]).astype(BF)
    store(o_proj, o_proj_h)
    arrived(g_z)
    dh[s_rows(), :] = z_total(pg, rgz).astype(BF)
    g_az = {dz: sems.start(dh.at[s_rows()], dh.at[s_rows()], s_dev(dz, 0)) for dz in (2, 1, 3)}
    g_ay = [sems.start(dh.at[s_rows()], dh.at[s_rows()], s_dev(0, dy)) for dy in (2, 1, 3)]
    arrived(h_ag[2:])
    arrived(d_aa)
    o_down[...] = dot(h_s[...].T, d_state_f[...]).astype(BF)
    store(o_down, o_down_h)
    for dz in (1, 3, 2):
        arrived([g_az[dz]])
        rows = s_rows(4 - dz)
        g_ay += [sems.start(dh.at[rows], dh.at[rows], s_dev(0, dy)) for dy in (2, 1, 3)]
    arrived(k_ay[2:])
    arrived(g_ay)
    for half in range(2):
        cols = pl.ds(half * N, N)
        dgu[:, cols] = (dh[...].astype(F32) * coef[:, cols].astype(F32)).astype(BF)
        store(dgu.at[:, cols], dgu_h.at[:, cols])

    for copy in sems.started:
        copy.wait_send()
    for copy in stores:
        copy.wait()


N_REMOTE = 160
N_LOCAL = 14 + 5


def results(
    xt_h, dgu_h, down_h, proj_h, o_gate_h, o_up_h, o_down_h, o_proj_h, xt, dgu, down, proj, out, sem
):
    gate, up = pl.ds(0, N), pl.ds(N, N)
    moves = [
        (xt_h, xt),
        (dgu_h.at[:, gate], dgu.at[:, gate]),
        (dgu_h.at[:, up], dgu.at[:, up]),
        (down_h, down),
        (proj_h, proj),
        (out.at[:, gate], o_gate_h),
        (out.at[:, up], o_up_h),
        (down, o_down_h),
        (proj, o_proj_h),
    ]
    copies = [
        pltpu.make_async_copy(src, dst, sem.at[index]) for index, (src, dst) in enumerate(moves)
    ]
    for copy in copies[:5]:
        copy.start()
    copies[0].wait()
    for half, cols in enumerate((gate, up)):
        copies[1 + half].wait()
        out[:, cols] = dot(xt[...], dgu[:, cols]).astype(BF)
        copies[5 + half].start()
        copies[3 + half].wait()
        copies[7 + half].start()
    for copy in copies[5:]:
        copy.wait()


def per_device(
    teacher_in, teacher_gain, teacher_gate, teacher_up, teacher_down, align_layer,
    student_in, student_gain, student_gate, student_up, student_down, projection,
):
    any_space = pl.BlockSpec(memory_space=pl.ANY)
    v = pltpu.VMEM
    scratch = [
        v((T, KT), BF), v((1, KT), F32), v((2 * KT, W2), BF), v((2 * N, KT), BF), v((1, T), jnp.int32),
        v((T, KS), BF), v((1, KS), F32), v((KS, W2), BF), v((4, N, KS), BF), v((4 * KS, KT), BF),
        v((64, 4 * KS), BF),
        v((T, KS), BF), v((KS, T), BF), v((T, 2 * KT), BF), v((T, 128), F32), v((T, N), BF),
        v((T, WS), BF), v((2, 32, WS), BF), v((2, 32, WS), BF), v((2, 64, WS), BF),
        v((3, 16, WS), BF), v((3, 16, WS), BF),
        v((T, N), BF), v((T, W2), BF),
        v((T, WS), BF), v((T // 2, WS), BF), v((T, WS), BF), v((7, 16, WS), BF),
        v((T, KT), BF), v((3, 64, KT), BF),
        v((64, 4 * KS), BF), v((15, 16, KS), BF), v((64, 4 * KS), BF),
        v((64, KT), BF), v((3, 16, KT), BF), v((T, KT), BF),
        v((64, 4 * KS), BF), v((15, 16, KS), BF), v((64, 4 * KS), BF),
        v((64, N), BF), v((3, 16, N), BF), v((T, N), BF), v((T, W2), BF),
        v((T, KS), BF), v((T, KS), BF),
        v((N, KS), BF), v((KS, KT), BF),
        pltpu.SemaphoreType.DMA((N_REMOTE,)),
        pltpu.SemaphoreType.DMA((N_REMOTE,)),
        pltpu.SemaphoreType.DMA((N_LOCAL,)),
    ]
    out = [
        jax.ShapeDtypeStruct((KS, T), BF),
        jax.ShapeDtypeStruct((T, W2), BF),
        jax.ShapeDtypeStruct((N, KS), BF),
        jax.ShapeDtypeStruct((KS, KT), BF),
    ]
    held = pl.pallas_call(
        kernel,
        name="distill",
        out_shape=out,
        in_specs=[any_space] * 12,
        out_specs=[any_space] * 4,
        scratch_shapes=scratch,
        cost_estimate=pl.CostEstimate(flops=3 * 10**9, bytes_accessed=10**7, transcendentals=10**5),
        compiler_params=pltpu.CompilerParams(
            collective_id=0, has_side_effects=True, vmem_limit_bytes=60 * 2**20
        ),
    )(
        teacher_in, teacher_gain.reshape(1, KT), teacher_gate, teacher_up,
        teacher_down.reshape(2 * N, KT), align_layer.reshape(1, T),
        student_in, student_gain.reshape(1, KS), student_gate, student_up, student_down, projection,
    )
    return pl.pallas_call(
        results,
        name="results",
        out_shape=[
            jax.ShapeDtypeStruct((KS, N), BF),
            jax.ShapeDtypeStruct((KS, N), BF),
            jax.ShapeDtypeStruct((N, KS), BF),
            jax.ShapeDtypeStruct((KS, KT), BF),
        ],
        in_specs=[any_space] * 4,
        out_specs=[any_space] * 4,
        scratch_shapes=[
            v((KS, T), BF), v((T, W2), BF), v((N, KS), BF), v((KS, KT), BF),
            v((KS, W2), BF), pltpu.SemaphoreType.DMA((9,)),
        ],
        cost_estimate=pl.CostEstimate(flops=3 * 10**8, bytes_accessed=4 * 10**6, transcendentals=0),
        compiler_params=pltpu.CompilerParams(vmem_limit_bytes=60 * 2**20),
    )(*held)


def solution(mesh):
    in_specs = (
        P(None, ("grp", "tp")),
        P(("grp", "tp")),
        P(None, ("grp", "tp"), "seq"),
        P(None, ("grp", "tp"), "seq"),
        P(None, "seq", ("grp", "tp")),
        P(),
        P(None, "seq"),
        P("seq"),
        P("seq", ("grp", "tp")),
        P("seq", ("grp", "tp")),
        P(("grp", "tp"), "seq"),
        P("seq", ("grp", "tp")),
    )
    out_specs = (
        P("seq", ("grp", "tp")),
        P("seq", ("grp", "tp")),
        P(("grp", "tp"), "seq"),
        P("seq", ("grp", "tp")),
    )
    return jax.shard_map(
        per_device, mesh=mesh, in_specs=in_specs, out_specs=out_specs, check_vma=False
    )
```

```python
import functools
import math

import jax
import jax.numpy as jnp
from jax import lax
from jax.experimental import pallas as pl
from jax.experimental.pallas import tpu as pltpu
from jax.sharding import PartitionSpec as P

MESH = pl.DeviceIdType.MESH
BF = jnp.bfloat16
F32 = jnp.float32

T = 256
DT = 8192
DS = 4096
KT = 512
KS = 256
N = 896
W2 = 2 * N
WS = W2 + 128

GOFF = [
    (a, b, c) for b in (2, 1, 3, 0) for a in (1, 0) for c in (1, 0) if (a, b, c) != (0, 0, 0)
]


def dot(a, b):
    return lax.dot_general(a, b, (((1,), (0,)), ((), ())), preferred_element_type=F32)


def dot_nt(a, b):
    return lax.dot_general(a, b, (((1,), (1,)), ((), ())), preferred_element_type=F32)


CHIPS = [o for o in GOFF if o[2] == 0]


class Sems:
    def __init__(self, send, recv):
        self.send, self.recv, self.started = send, recv, []

    def start(self, src, dst, device):
        index = len(self.started)
        copy = pltpu.make_async_remote_copy(
            src_ref=src,
            dst_ref=dst,
            send_sem=self.send.at[index],
            recv_sem=self.recv.at[index],
            device_id=device,
            device_id_type=MESH,
        )
        copy.start()
        self.started.append(copy)
        return copy


def squares(total):
    rows = total.shape[0]
    wide = jnp.broadcast_to(total, (rows, 128))
    high = wide.astype(BF)
    low = (wide - high.astype(F32)).astype(BF)
    lane = lax.broadcasted_iota(jnp.int32, (rows, 128), 1)
    return jnp.where(lane < 64, high.astype(F32), low.astype(F32)).astype(BF)


def total_of(columns):
    lane = lax.broadcasted_iota(jnp.int32, columns.shape, 1)
    picked = jnp.where((lane == 0) | (lane == 64), columns, 0.0)
    return jnp.sum(picked, axis=1, keepdims=True)


def kernel(
    t_in_h, t_gain_h, t_gate_h, t_up_h, t_down_h, align_h,
    s_in_h, s_gain_h, s_gate_h, s_up_h, s_down_h, proj_h,
    xt_h, dgu_h, o_down_h, o_proj_h,
    t_in, t_gain, t_w, t_down, align,
    s_in, s_gain, s_w, down, proj, s_tok,
    xg, xgt, xt, hm, h_t,
    pb, rfar, bsum, rby, zb, rbz, h_s, coef,
    pc, rcore, pcore, rc, tp, rt, pd, rd, state,
    pe, rez, dp, pf, rf, d_state,
    pg, rgz, dh, dgu, state_f, d_state_f,
    o_down, o_proj,
    send, recv, lsem,
):
    grp, seq, tpi = lax.axis_index("grp"), lax.axis_index("seq"), lax.axis_index("tp")
    zh, y = seq // 4, seq % 4
    x, core = tpi // 2, tpi % 2

    def s_dev(dz, dy):
        return (grp, ((zh + dz) % 4) * 4 + (y + dy) % 4, tpi)

    def g_dev(a, b, c):
        return ((grp + a) % 2, seq, ((x + b) % 4) * 2 + (core + c) % 2)

    def g_rows(a=0, b=0, c=0):
        owner = ((core + c) % 2) * 8 + ((grp + a) % 2) * 4 + (x + b) % 4
        return pl.ds(pl.multiple_of(owner * 16, 16), 16)

    def half_rows(c=0):
        return pl.ds(pl.multiple_of(((core + c) % 2) * 128, 128), 128)

    def g_block(a=0, b=0, c=0):
        row = ((core + c) % 2) * 2 + (grp + a) % 2
        return (
            pl.ds(pl.multiple_of(row * 16, 16), 16),
            pl.ds(pl.multiple_of(((x + b) % 4) * KS, KS), KS),
        )

    def s_rows(dz=0, dy=0):
        owner = ((y + dy) % 4) * 4 + (zh + dz) % 4
        return pl.ds(pl.multiple_of(owner * 16, 16), 16)

    def y_rows(dy=0):
        return pl.ds(pl.multiple_of(((y + dy) % 4) * 64, 64), 64)

    def y_half(dy, half):
        return pl.ds(pl.multiple_of(((y + dy) % 4) * 64 + half * 32, 32), 32)

    def z_rows(dz=0):
        return pl.ds(pl.multiple_of(((zh + dz) % 4) * 16, 16), 16)

    def feat(dy=0, start=0, count=KS):
        return pl.ds(pl.multiple_of(((y + dy) % 4) * KS + start, 128), count)

    sems = Sems(send, recv)
    loads = []

    def load(src, dst):
        copy = pltpu.make_async_copy(src, dst, lsem.at[len(loads)])
        copy.start()
        loads.append(copy)
        return copy

    def arrived(copies):
        for copy in copies:
            copy.wait_recv()

    l_sd = load(s_down_h, down.at[y])
    l_s = [
        load(s_in_h, s_in),
        load(s_gain_h, s_gain),
        load(s_gate_h, s_w.at[:, pl.ds(0, N)]),
        load(s_up_h, s_w.at[:, pl.ds(N, N)]),
    ]
    barrier = pltpu.get_barrier_semaphore()
    partners = [s_dev(0, k) for k in (1, 2, 3)] + [s_dev(k, 0) for k in (1, 2, 3)]
    partners += [g_dev(*o) for o in GOFF]
    for device in partners:
        pl.semaphore_signal(barrier, inc=1, device_id=device, device_id_type=MESH)

    def y_sum(src, slots, dz, columns):
        total = src[s_rows(dz), columns].astype(F32)
        for index in range(2):
            total = total + slots[index, z_rows(dz), columns].astype(F32)
        return total

    def rs_z(src, slots):
        return [
            sems.start(src.at[z_rows(dz)], slots.at[dz - 1], s_dev(dz, 0)) for dz in (2, 1, 3)
        ]

    def z_total(src, slots):
        total = src[z_rows(), :].astype(F32)
        for index in range(3):
            total = total + slots[index].astype(F32)
        return total

    def ag_z(buf):
        return [sems.start(buf.at[s_rows()], buf.at[s_rows()], s_dev(dz, 0)) for dz in (2, 1, 3)]

    def to_y(src, dst):
        return [sems.start(src(dy), dst(dy), s_dev(0, dy)) for dy in (2, 1, 3)]

    def rs_g(src, slots):
        return [
            sems.start(src.at[g_block(*o)], slots.at[i], g_dev(*o)) for i, o in enumerate(GOFF)
        ]

    def ag_g(buf):
        return [sems.start(buf.at[g_block()], buf.at[g_block()], g_dev(*o)) for o in GOFF]

    def g_total(src, slots):
        total = src[g_block()].astype(F32)
        for index in range(15):
            total = total + slots[index].astype(F32)
        return total

    def neighbours(src, dst):
        return [sems.start(src, dst, s_dev(0, dy)) for dy in (1, 3)]

    def proj_half(dy, half):
        return proj.at[feat(dy, half * 128, 128), :]

    def down_half(dy, half):
        return down.at[(y + dy) % 4, pl.ds(half * (N // 2), N // 2), :]

    def ag_y(buf):
        return neighbours(buf.at[y_rows()], buf.at[y_rows()])

    def relay_rows(copies, buf):
        return relay(copies, lambda dy, half: buf.at[y_half(dy, half)])

    def half_to(part, on):
        return [
            sems.start(part(0, 1 - on), part(0, 1 - on), s_dev(0, 1)),
            sems.start(part(0, on), part(0, on), s_dev(0, 3)),
        ]

    def relay(copies, part):
        arrived(copies)
        return [
            sems.start(part(3, 0), part(3, 0), s_dev(0, 1)),
            sems.start(part(1, 1), part(1, 1), s_dev(0, 3)),
        ]


    for copy in l_s[:2]:
        copy.wait()
    wide = s_in[...].astype(F32)
    xg[...] = (wide * s_gain[...]).astype(BF)
    pb[:, W2:] = squares(jnp.sum(wide * wide, axis=1, keepdims=True))
    for copy in l_s[2:]:
        copy.wait()
    l_t = [load(t_in_h, t_in), load(t_gain_h, t_gain), load(align_h, align)]
    for layer in range(2):
        rows = pl.ds(layer * KT, KT)
        l_t.append(load(t_gate_h.at[layer], t_w.at[rows, pl.ds(0, N)]))
        l_t.append(load(t_up_h.at[layer], t_w.at[rows, pl.ds(N, N)]))
    l_p = load(proj_h, proj.at[feat(), :])
    l_td = load(t_down_h, t_down)
    for tile in range(7):
        cols = pl.ds(tile * 256, 256)
        pb[:, cols] = dot(xg[...], s_w[:, cols]).astype(BF)

    pl.semaphore_wait(barrier, len(partners))
    b_far = [
        sems.start(pb.at[y_half(2, 0)], rfar.at[0], s_dev(0, 1)),
        sems.start(pb.at[y_half(2, 1)], rfar.at[1], s_dev(0, 3)),
    ]
    l_sd.wait()
    w_down = half_to(down_half, 1)
    b_y = [
        sems.start(pb.at[y_half(1, 1)], rby.at[0, pl.ds(32, 32)], s_dev(0, 1)),
        sems.start(pb.at[y_half(3, 0)], rby.at[1, pl.ds(0, 32)], s_dev(0, 3)),
    ]

    for copy in l_t:
        copy.wait()
    diagonal = lax.broadcasted_iota(jnp.int32, (T, T), 0) == lax.broadcasted_iota(
        jnp.int32, (T, T), 1
    )
    layer_of = jnp.sum(
        jnp.where(diagonal, jnp.broadcast_to(align[...].astype(F32), (T, T)), 0.0),
        axis=1,
        keepdims=True,
    )
    hm[...] = jnp.broadcast_to(layer_of, (T, 128))
    wide = t_in[...].astype(F32)
    scaled = wide * t_gain[...]
    xt[:, :KT] = jnp.where(layer_of < 0.5, scaled, 0.0).astype(BF)
    xt[:, KT:] = jnp.where(layer_of < 0.5, 0.0, scaled).astype(BF)
    pc[:, W2:] = squares(jnp.sum(wide * wide, axis=1, keepdims=True))

    for tile in range(7):
        cols = pl.ds(tile * 256, 256)
        pc[:, cols] = dot(xt[...], t_w[:, cols]).astype(BF)

    c_core = sems.start(pc.at[half_rows(1)], rcore, g_dev(0, 0, 1))
    xgt[...] = xg[...].T
    for half, dy in ((0, 1), (1, 3)):
        arrived([b_far[half]])
        rows = y_half(dy, half)
        both = pb[rows, :W2].astype(F32) + rfar[half, :, :W2].astype(F32)
        bsum[half, :, :W2] = both.astype(BF)
        both = total_of(pb[rows, W2:].astype(F32) + rfar[half, :, W2:].astype(F32))
        bsum[half, :, W2:] = squares(both)
        slot = rby.at[half, pl.ds(half * 32, 32)]
        b_y.append(sems.start(bsum.at[half], slot, s_dev(0, dy)))
    w_down += relay(w_down, down_half)
    l_p.wait()
    arrived([c_core])
    pair = pc[half_rows(), :W2].astype(F32) + rcore[:, :W2].astype(F32)
    pcore[half_rows(), :W2] = pair.astype(BF)
    pair = total_of(pc[half_rows(), W2:].astype(F32) + rcore[:, W2:].astype(F32))
    pcore[half_rows(), W2:] = squares(pair)
    w_down += half_to(down_half, 0)
    c_rs = [sems.start(pcore.at[g_rows(*o)], rc.at[i], g_dev(*o)) for i, o in enumerate(CHIPS)]

    def c_total(columns):
        total = pcore[g_rows(), columns].astype(F32)
        for index in range(7):
            total = total + rc[index, :, columns].astype(F32)
        return total

    b_z = []
    arrived(b_y)
    for dz in (2, 1, 3):
        zb[dz - 1, :, :W2] = y_sum(pb, rby, dz, pl.ds(0, W2)).astype(BF)
        zb[dz - 1, :, W2:] = squares(total_of(y_sum(pb, rby, dz, pl.ds(W2, 128))))
        b_z.append(sems.start(zb.at[dz - 1], rbz.at[dz - 1], s_dev(dz, 0)))
    w_proj = neighbours(proj.at[feat(), :], proj.at[feat(), :])
    w_tok = to_y(lambda dy: s_in.at[y_rows(dy)], lambda dy: s_tok.at[:, feat()])
    s_tok[:, feat()] = s_in[y_rows(), :]

    def b_total(columns):
        total = y_sum(pb, rby, 0, columns)
        for index in range(3):
            total = total + rbz[index, :, columns].astype(F32)
        return total

    arrived(b_z)
    scale = lax.rsqrt(total_of(b_total(pl.ds(W2, 128))) / DS + 1e-05)
    g = b_total(pl.ds(0, N)) * scale
    u = b_total(pl.ds(N, N)) * scale
    q = jax.nn.sigmoid(g)
    h_s[s_rows(), :] = (g * q * u).astype(BF)
    b_ag = ag_z(h_s)
    coef[s_rows(), :N] = (scale * u * q * (1.0 + g * (1.0 - q))).astype(BF)
    coef[s_rows(), N:] = (scale * g * q).astype(BF)

    arrived(c_rs)
    scale = lax.rsqrt(total_of(c_total(pl.ds(W2, 128))) / DT + 1e-05)
    g = c_total(pl.ds(0, N)) * scale
    u = c_total(pl.ds(N, N)) * scale
    h_t[g_rows(), :] = (g * jax.nn.sigmoid(g) * u).astype(BF)
    c_ag = [sems.start(h_t.at[g_rows()], h_t.at[g_rows()], g_dev(*o)) for o in CHIPS]

    arrived(b_ag)
    arrived(w_down[2:])

    for tile in range(4):
        cols = pl.ds(tile * 256, 256)
        pd[:, cols] = dot(h_s[y_rows(), :], down[tile]).astype(BF)
    d_rs = rs_g(pd, rd)

    arrived(c_ag)
    c_core = sems.start(h_t.at[half_rows()], h_t.at[half_rows()], g_dev(0, 0, 1))
    w_proj += relay(w_proj, proj_half)
    l_td.wait()
    arrived([c_core])
    first = hm[:, 0:1] < 0.5
    zero = jnp.zeros((), BF)
    for half in range(2):
        cols = pl.ds(half * 256, 256)
        tp[:, cols] = (
            dot(jnp.where(first, h_t[...], zero), t_down[:N, cols])
            + dot(jnp.where(first, zero, h_t[...]), t_down[N:, cols])
        ).astype(BF)
    t_rs = to_y(lambda dy: tp.at[y_rows(dy)], lambda dy: rt.at[dy - 1])

    arrived(w_tok)
    arrived(d_rs)
    state[g_block()] = (s_tok[g_block()].astype(F32) + g_total(pd, rd)).astype(BF)
    d_ag = ag_g(state)
    k_ag = ag_z(coef)
    h_ag = ag_y(h_s)
    arrived(w_proj[2:])
    arrived(t_rs)
    arrived(d_ag)

    for half in range(2):
        cols = pl.ds(half * 256, 256)
        target = tp[y_rows(), cols].astype(F32)
        for index in range(3):
            target = target + rt[index, :, cols].astype(F32)
        pe[:, cols] = (dot(state[...], proj[:, cols]) - target).astype(BF)
    e_z = rs_z(pe, rez)
    s_aa = to_y(lambda dy: state.at[:, feat(dy)], lambda dy: state_f.at[y_rows()])
    state_f[y_rows(), :] = state[:, feat()]
    h_ag += relay_rows(h_ag, h_s)
    arrived(e_z)
    dp[s_rows(), :] = (
        (z_total(pe, rez) - t_in[s_rows(), :].astype(F32)) * (1.0 / math.sqrt(T))
    ).astype(BF)
    e_ag = ag_z(dp)
    arrived(k_ag)
    k_ay = ag_y(coef)
    arrived(e_ag)

    for tile in range(4):
        cols = pl.ds(tile * 256, 256)
        pf[:, cols] = dot_nt(dp[y_rows(), :], proj[cols, :]).astype(BF)
    f_rs = rs_g(pf, rf)
    p_ag = ag_y(dp)
    arrived(f_rs)
    d_state[g_block()] = g_total(pf, rf).astype(BF)
    f_ag = ag_g(d_state)
    p_ag += relay_rows(p_ag, dp)
    stores = []

    def store(src, dst):
        copy = pltpu.make_async_copy(src, dst, lsem.at[len(loads) + len(stores)])
        copy.start()
        stores.append(copy)

    store(xgt, xt_h)
    arrived(s_aa)
    state_t = state_f[...].T
    arrived(f_ag)

    d_hidden = dot_nt(d_state[:, :KS], down[0])
    for tile in range(1, 4):
        d_hidden += dot_nt(d_state[:, tile * KS : (tile + 1) * KS], down[tile])
    pg[...] = d_hidden.astype(BF)
    g_z = rs_z(pg, rgz)
    k_ay += relay_rows(k_ay, coef)
    d_aa = to_y(lambda dy: d_state.at[:, feat(dy)], lambda dy: d_state_f.at[y_rows()])
    d_state_f[y_rows(), :] = d_state[:, feat()]
    arrived(p_ag[2:])
    o_proj[...] = dot(state_t, dp[...]).astype(BF)
    store(o_proj, o_proj_h)
    arrived(g_z)
    dh[s_rows(), :] = z_total(pg, rgz).astype(BF)
    g_az = {dz: sems.start(dh.at[s_rows()], dh.at[s_rows()], s_dev(dz, 0)) for dz in (2, 1, 3)}
    g_ay = [sems.start(dh.at[s_rows()], dh.at[s_rows()], s_dev(0, dy)) for dy in (2, 1, 3)]
    arrived(h_ag[2:])
    arrived(d_aa)
    o_down[...] = dot(h_s[...].T, d_state_f[...]).astype(BF)
    store(o_down, o_down_h)
    for dz in (1, 3, 2):
        arrived([g_az[dz]])
        rows = s_rows(4 - dz)
        g_ay += [sems.start(dh.at[rows], dh.at[rows], s_dev(0, dy)) for dy in (2, 1, 3)]
    arrived(k_ay[2:])
    arrived(g_ay)
    for half in range(2):
        cols = pl.ds(half * N, N)
        dgu[:, cols] = (dh[...].astype(F32) * coef[:, cols].astype(F32)).astype(BF)
        store(dgu.at[:, cols], dgu_h.at[:, cols])

    for copy in sems.started:
        copy.wait_send()
    for copy in stores:
        copy.wait()


N_REMOTE = 160
N_LOCAL = 14 + 5


def results(
    xt_h, dgu_h, down_h, proj_h, o_gate_h, o_up_h, o_down_h, o_proj_h, xt, dgu, down, proj, out, sem
):
    gate, up = pl.ds(0, N), pl.ds(N, N)
    moves = [
        (xt_h, xt),
        (dgu_h.at[:, gate], dgu.at[:, gate]),
        (dgu_h.at[:, up], dgu.at[:, up]),
        (down_h, down),
        (proj_h, proj),
        (out.at[:, gate], o_gate_h),
        (out.at[:, up], o_up_h),
        (down, o_down_h),
        (proj, o_proj_h),
    ]
    copies = [
        pltpu.make_async_copy(src, dst, sem.at[index]) for index, (src, dst) in enumerate(moves)
    ]
    for copy in copies[:5]:
        copy.start()
    copies[0].wait()
    for half, cols in enumerate((gate, up)):
        copies[1 + half].wait()
        out[:, cols] = dot(xt[...], dgu[:, cols]).astype(BF)
        copies[5 + half].start()
        copies[3 + half].wait()
        copies[7 + half].start()
    for copy in copies[5:]:
        copy.wait()


def per_device(
    teacher_in, teacher_gain, teacher_gate, teacher_up, teacher_down, align_layer,
    student_in, student_gain, student_gate, student_up, student_down, projection,
):
    any_space = pl.BlockSpec(memory_space=pl.ANY)
    v = pltpu.VMEM
    scratch = [
        v((T, KT), BF), v((1, KT), F32), v((2 * KT, W2), BF), v((2 * N, KT), BF), v((1, T), jnp.int32),
        v((T, KS), BF), v((1, KS), F32), v((KS, W2), BF), v((4, N, KS), BF), v((4 * KS, KT), BF),
        v((64, 4 * KS), BF),
        v((T, KS), BF), v((KS, T), BF), v((T, 2 * KT), BF), v((T, 128), F32), v((T, N), BF),
        v((T, WS), BF), v((2, 32, WS), BF), v((2, 32, WS), BF), v((2, 64, WS), BF),
        v((3, 16, WS), BF), v((3, 16, WS), BF),
        v((T, N), BF), v((T, W2), BF),
        v((T, WS), BF), v((T // 2, WS), BF), v((T, WS), BF), v((7, 16, WS), BF),
        v((T, KT), BF), v((3, 64, KT), BF),
        v((64, 4 * KS), BF), v((15, 16, KS), BF), v((64, 4 * KS), BF),
        v((64, KT), BF), v((3, 16, KT), BF), v((T, KT), BF),
        v((64, 4 * KS), BF), v((15, 16, KS), BF), v((64, 4 * KS), BF),
        v((64, N), BF), v((3, 16, N), BF), v((T, N), BF), v((T, W2), BF),
        v((T, KS), BF), v((T, KS), BF),
        v((N, KS), BF), v((KS, KT), BF),
        pltpu.SemaphoreType.DMA((N_REMOTE,)),
        pltpu.SemaphoreType.DMA((N_REMOTE,)),
        pltpu.SemaphoreType.DMA((N_LOCAL,)),
    ]
    out = [
        jax.ShapeDtypeStruct((KS, T), BF),
        jax.ShapeDtypeStruct((T, W2), BF),
        jax.ShapeDtypeStruct((N, KS), BF),
        jax.ShapeDtypeStruct((KS, KT), BF),
    ]
    held = pl.pallas_call(
        kernel,
        name="distill",
        out_shape=out,
        in_specs=[any_space] * 12,
        out_specs=[any_space] * 4,
        scratch_shapes=scratch,
        cost_estimate=pl.CostEstimate(flops=3 * 10**9, bytes_accessed=10**7, transcendentals=10**5),
        compiler_params=pltpu.CompilerParams(
            collective_id=0, has_side_effects=True, vmem_limit_bytes=60 * 2**20
        ),
    )(
        teacher_in, teacher_gain.reshape(1, KT), teacher_gate, teacher_up,
        teacher_down.reshape(2 * N, KT), align_layer.reshape(1, T),
        student_in, student_gain.reshape(1, KS), student_gate, student_up, student_down, projection,
    )
    return pl.pallas_call(
        results,
        name="results",
        out_shape=[
            jax.ShapeDtypeStruct((KS, N), BF),
            jax.ShapeDtypeStruct((KS, N), BF),
            jax.ShapeDtypeStruct((N, KS), BF),
            jax.ShapeDtypeStruct((KS, KT), BF),
        ],
        in_specs=[any_space] * 4,
        out_specs=[any_space] * 4,
        scratch_shapes=[
            v((KS, T), BF), v((T, W2), BF), v((N, KS), BF), v((KS, KT), BF),
            v((KS, W2), BF), pltpu.SemaphoreType.DMA((9,)),
        ],
        cost_estimate=pl.CostEstimate(flops=3 * 10**8, bytes_accessed=4 * 10**6, transcendentals=0),
        compiler_params=pltpu.CompilerParams(vmem_limit_bytes=60 * 2**20),
    )(*held)


def solution(mesh):
    in_specs = (
        P(None, ("grp", "tp")),
        P(("grp", "tp")),
        P(None, ("grp", "tp"), "seq"),
        P(None, ("grp", "tp"), "seq"),
        P(None, "seq", ("grp", "tp")),
        P(),
        P(None, "seq"),
        P("seq"),
        P("seq", ("grp", "tp")),
        P("seq", ("grp", "tp")),
        P(("grp", "tp"), "seq"),
        P("seq", ("grp", "tp")),
    )
    out_specs = (
        P("seq", ("grp", "tp")),
        P("seq", ("grp", "tp")),
        P(("grp", "tp"), "seq"),
        P("seq", ("grp", "tp")),
    )
    return jax.shard_map(
        per_device, mesh=mesh, in_specs=in_specs, out_specs=out_specs, check_vma=False
    )
```

```python
import functools
import math

import jax
import jax.numpy as jnp
from jax import lax
from jax.experimental import pallas as pl
from jax.experimental.pallas import tpu as pltpu
from jax.sharding import PartitionSpec as P

MESH = pl.DeviceIdType.MESH
BF = jnp.bfloat16
F32 = jnp.float32

T = 256
DT = 8192
DS = 4096
KT = 512
KS = 256
N = 896
W2 = 2 * N
WS = W2 + 128

GOFF = [
    (a, b, c) for b in (2, 1, 3, 0) for a in (1, 0) for c in (1, 0) if (a, b, c) != (0, 0, 0)
]


def dot(a, b):
    return lax.dot_general(a, b, (((1,), (0,)), ((), ())), preferred_element_type=F32)


def dot_nt(a, b):
    return lax.dot_general(a, b, (((1,), (1,)), ((), ())), preferred_element_type=F32)


CHIPS = [o for o in GOFF if o[2] == 0]


class Sems:
    def __init__(self, send, recv):
        self.send, self.recv, self.started = send, recv, []

    def start(self, src, dst, device):
        index = len(self.started)
        copy = pltpu.make_async_remote_copy(
            src_ref=src,
            dst_ref=dst,
            send_sem=self.send.at[index],
            recv_sem=self.recv.at[index],
            device_id=device,
            device_id_type=MESH,
        )
        copy.start()
        self.started.append(copy)
        return copy


def squares(total):
    rows = total.shape[0]
    wide = jnp.broadcast_to(total, (rows, 128))
    high = wide.astype(BF)
    low = (wide - high.astype(F32)).astype(BF)
    lane = lax.broadcasted_iota(jnp.int32, (rows, 128), 1)
    return jnp.where(lane < 64, high.astype(F32), low.astype(F32)).astype(BF)


def total_of(columns):
    lane = lax.broadcasted_iota(jnp.int32, columns.shape, 1)
    picked = jnp.where((lane == 0) | (lane == 64), columns, 0.0)
    return jnp.sum(picked, axis=1, keepdims=True)


def kernel(
    t_in_h, t_gain_h, t_gate_h, t_up_h, t_down_h, align_h,
    s_in_h, s_gain_h, s_gate_h, s_up_h, s_down_h, proj_h,
    xt_h, dgu_h, o_down_h, o_proj_h,
    t_in, t_gain, t_w, t_down, align,
    s_in, s_gain, s_w, down, proj, s_tok,
    xg, xgt, xt, hm, h_t,
    pb, rfar, bsum, rby, zb, rbz, h_s, coef,
    pc, rcore, pcore, rc, tp, rt, pd, rd, state,
    pe, rez, dp, pf, rf, d_state,
    pg, rgz, dh, dgu, state_f, d_state_f,
    o_down, o_proj,
    send, recv, lsem,
):
    grp, seq, tpi = lax.axis_index("grp"), lax.axis_index("seq"), lax.axis_index("tp")
    zh, y = seq // 4, seq % 4
    x, core = tpi // 2, tpi % 2

    def s_dev(dz, dy):
        return (grp, ((zh + dz) % 4) * 4 + (y + dy) % 4, tpi)

    def g_dev(a, b, c):
        return ((grp + a) % 2, seq, ((x + b) % 4) * 2 + (core + c) % 2)

    def g_rows(a=0, b=0, c=0):
        owner = ((core + c) % 2) * 8 + ((grp + a) % 2) * 4 + (x + b) % 4
        return pl.ds(pl.multiple_of(owner * 16, 16), 16)

    def half_rows(c=0):
        return pl.ds(pl.multiple_of(((core + c) % 2) * 128, 128), 128)

    def g_block(a=0, b=0, c=0):
        row = ((core + c) % 2) * 2 + (grp + a) % 2
        return (
            pl.ds(pl.multiple_of(row * 16, 16), 16),
            pl.ds(pl.multiple_of(((x + b) % 4) * KS, KS), KS),
        )

    def s_rows(dz=0, dy=0):
        owner = ((y + dy) % 4) * 4 + (zh + dz) % 4
        return pl.ds(pl.multiple_of(owner * 16, 16), 16)

    def y_rows(dy=0):
        return pl.ds(pl.multiple_of(((y + dy) % 4) * 64, 64), 64)

    def y_half(dy, half):
        return pl.ds(pl.multiple_of(((y + dy) % 4) * 64 + half * 32, 32), 32)

    def z_rows(dz=0):
        return pl.ds(pl.multiple_of(((zh + dz) % 4) * 16, 16), 16)

    def feat(dy=0, start=0, count=KS):
        return pl.ds(pl.multiple_of(((y + dy) % 4) * KS + start, 128), count)

    sems = Sems(send, recv)
    loads = []

    def load(src, dst):
        copy = pltpu.make_async_copy(src, dst, lsem.at[len(loads)])
        copy.start()
        loads.append(copy)
        return copy

    def arrived(copies):
        for copy in copies:
            copy.wait_recv()

    l_sd = load(s_down_h, down.at[y])
    l_s = [
        load(s_in_h, s_in),
        load(s_gain_h, s_gain),
        load(s_gate_h, s_w.at[:, pl.ds(0, N)]),
        load(s_up_h, s_w.at[:, pl.ds(N, N)]),
    ]
    barrier = pltpu.get_barrier_semaphore()
    partners = [s_dev(0, k) for k in (1, 2, 3)] + [s_dev(k, 0) for k in (1, 2, 3)]
    partners += [g_dev(*o) for o in GOFF]
    for device in partners:
        pl.semaphore_signal(barrier, inc=1, device_id=device, device_id_type=MESH)

    def y_sum(src, slots, dz, columns):
        total = src[s_rows(dz), columns].astype(F32)
        for index in range(2):
            total = total + slots[index, z_rows(dz), columns].astype(F32)
        return total

    def rs_z(src, slots):
        return [
            sems.start(src.at[z_rows(dz)], slots.at[dz - 1], s_dev(dz, 0)) for dz in (2, 1, 3)
        ]

    def z_total(src, slots):
        total = src[z_rows(), :].astype(F32)
        for index in range(3):
            total = total + slots[index].astype(F32)
        return total

    def ag_z(buf):
        return [sems.start(buf.at[s_rows()], buf.at[s_rows()], s_dev(dz, 0)) for dz in (2, 1, 3)]

    def to_y(src, dst):
        return [sems.start(src(dy), dst(dy), s_dev(0, dy)) for dy in (2, 1, 3)]

    def rs_g(src, slots):
        return [
            sems.start(src.at[g_block(*o)], slots.at[i], g_dev(*o)) for i, o in enumerate(GOFF)
        ]

    def ag_g(buf):
        return [sems.start(buf.at[g_block()], buf.at[g_block()], g_dev(*o)) for o in GOFF]

    def g_total(src, slots):
        total = src[g_block()].astype(F32)
        for index in range(15):
            total = total + slots[index].astype(F32)
        return total

    def neighbours(src, dst):
        return [sems.start(src, dst, s_dev(0, dy)) for dy in (1, 3)]

    def proj_half(dy, half):
        return proj.at[feat(dy, half * 128, 128), :]

    def down_half(dy, half):
        return down.at[(y + dy) % 4, pl.ds(half * (N // 2), N // 2), :]

    def ag_y(buf):
        return neighbours(buf.at[y_rows()], buf.at[y_rows()])

    def relay_rows(copies, buf):
        return relay(copies, lambda dy, half: buf.at[y_half(dy, half)])

    def half_to(part, on):
        return [
            sems.start(part(0, 1 - on), part(0, 1 - on), s_dev(0, 1)),
            sems.start(part(0, on), part(0, on), s_dev(0, 3)),
        ]

    def relay(copies, part):
        arrived(copies)
        return [
            sems.start(part(3, 0), part(3, 0), s_dev(0, 1)),
            sems.start(part(1, 1), part(1, 1), s_dev(0, 3)),
        ]


    for copy in l_s[:2]:
        copy.wait()
    wide = s_in[...].astype(F32)
    xg[...] = (wide * s_gain[...]).astype(BF)
    pb[:, W2:] = squares(jnp.sum(wide * wide, axis=1, keepdims=True))
    for copy in l_s[2:]:
        copy.wait()
    l_t = [load(t_in_h, t_in), load(t_gain_h, t_gain), load(align_h, align)]
    for layer in range(2):
        rows = pl.ds(layer * KT, KT)
        l_t.append(load(t_gate_h.at[layer], t_w.at[rows, pl.ds(0, N)]))
        l_t.append(load(t_up_h.at[layer], t_w.at[rows, pl.ds(N, N)]))
    l_p = load(proj_h, proj.at[feat(), :])
    l_td = load(t_down_h, t_down)
    for tile in range(7):
        cols = pl.ds(tile * 256, 256)
        pb[:, cols] = dot(xg[...], s_w[:, cols]).astype(BF)

    pl.semaphore_wait(barrier, len(partners))
    b_far = [
        sems.start(pb.at[y_half(2, 0)], rfar.at[0], s_dev(0, 1)),
        sems.start(pb.at[y_half(2, 1)], rfar.at[1], s_dev(0, 3)),
    ]
    l_sd.wait()
    w_down = half_to(down_half, 1)
    b_y = [
        sems.start(pb.at[y_half(1, 1)], rby.at[0, pl.ds(32, 32)], s_dev(0, 1)),
        sems.start(pb.at[y_half(3, 0)], rby.at[1, pl.ds(0, 32)], s_dev(0, 3)),
    ]

    for copy in l_t:
        copy.wait()
    diagonal = lax.broadcasted_iota(jnp.int32, (T, T), 0) == lax.broadcasted_iota(
        jnp.int32, (T, T), 1
    )
    layer_of = jnp.sum(
        jnp.where(diagonal, jnp.broadcast_to(align[...].astype(F32), (T, T)), 0.0),
        axis=1,
        keepdims=True,
    )
    hm[...] = jnp.broadcast_to(layer_of, (T, 128))
    wide = t_in[...].astype(F32)
    scaled = wide * t_gain[...]
    xt[:, :KT] = jnp.where(layer_of < 0.5, scaled, 0.0).astype(BF)
    xt[:, KT:] = jnp.where(layer_of < 0.5, 0.0, scaled).astype(BF)
    pc[:, W2:] = squares(jnp.sum(wide * wide, axis=1, keepdims=True))

    for tile in range(7):
        cols = pl.ds(tile * 256, 256)
        pc[:, cols] = dot(xt[...], t_w[:, cols]).astype(BF)

    c_core = sems.start(pc.at[half_rows(1)], rcore, g_dev(0, 0, 1))
    xgt[...] = xg[...].T
    for half, dy in ((0, 1), (1, 3)):
        arrived([b_far[half]])
        rows = y_half(dy, half)
        both = pb[rows, :W2].astype(F32) + rfar[half, :, :W2].astype(F32)
        bsum[half, :, :W2] = both.astype(BF)
        both = total_of(pb[rows, W2:].astype(F32) + rfar[half, :, W2:].astype(F32))
        bsum[half, :, W2:] = squares(both)
        slot = rby.at[half, pl.ds(half * 32, 32)]
        b_y.append(sems.start(bsum.at[half], slot, s_dev(0, dy)))
    w_down += relay(w_down, down_half)
    l_p.wait()
    arrived([c_core])
    pair = pc[half_rows(), :W2].astype(F32) + rcore[:, :W2].astype(F32)
    pcore[half_rows(), :W2] = pair.astype(BF)
    pair = total_of(pc[half_rows(), W2:].astype(F32) + rcore[:, W2:].astype(F32))
    pcore[half_rows(), W2:] = squares(pair)
    w_down += half_to(down_half, 0)
    c_rs = [sems.start(pcore.at[g_rows(*o)], rc.at[i], g_dev(*o)) for i, o in enumerate(CHIPS)]

    def c_total(columns):
        total = pcore[g_rows(), columns].astype(F32)
        for index in range(7):
            total = total + rc[index, :, columns].astype(F32)
        return total

    b_z = []
    arrived(b_y)
    for dz in (2, 1, 3):
        zb[dz - 1, :, :W2] = y_sum(pb, rby, dz, pl.ds(0, W2)).astype(BF)
        zb[dz - 1, :, W2:] = squares(total_of(y_sum(pb, rby, dz, pl.ds(W2, 128))))
        b_z.append(sems.start(zb.at[dz - 1], rbz.at[dz - 1], s_dev(dz, 0)))
    w_proj = half_to(proj_half, 1)
    w_tok = to_y(lambda dy: s_in.at[y_rows(dy)], lambda dy: s_tok.at[:, feat()])
    s_tok[:, feat()] = s_in[y_rows(), :]

    def b_total(columns):
        total = y_sum(pb, rby, 0, columns)
        for index in range(3):
            total = total + rbz[index, :, columns].astype(F32)
        return total

    arrived(b_z)
    scale = lax.rsqrt(total_of(b_total(pl.ds(W2, 128))) / DS + 1e-05)
    g = b_total(pl.ds(0, N)) * scale
    u = b_total(pl.ds(N, N)) * scale
    q = jax.nn.sigmoid(g)
    h_s[s_rows(), :] = (g * q * u).astype(BF)
    b_ag = ag_z(h_s)
    coef[s_rows(), :N] = (scale * u * q * (1.0 + g * (1.0 - q))).astype(BF)
    coef[s_rows(), N:] = (scale * g * q).astype(BF)

    arrived(c_rs)
    scale = lax.rsqrt(total_of(c_total(pl.ds(W2, 128))) / DT + 1e-05)
    g = c_total(pl.ds(0, N)) * scale
    u = c_total(pl.ds(N, N)) * scale
    h_t[g_rows(), :] = (g * jax.nn.sigmoid(g) * u).astype(BF)
    c_ag = [sems.start(h_t.at[g_rows()], h_t.at[g_rows()], g_dev(*o)) for o in CHIPS]

    arrived(b_ag)
    arrived(w_down[2:])

    for tile in range(4):
        cols = pl.ds(tile * 256, 256)
        pd[:, cols] = dot(h_s[y_rows(), :], down[tile]).astype(BF)
    d_rs = rs_g(pd, rd)

    arrived(c_ag)
    c_core = sems.start(h_t.at[half_rows()], h_t.at[half_rows()], g_dev(0, 0, 1))
    w_proj += relay(w_proj, proj_half)
    w_proj += half_to(proj_half, 0)
    l_td.wait()
    arrived([c_core])
    first = hm[:, 0:1] < 0.5
    zero = jnp.zeros((), BF)
    for half in range(2):
        cols = pl.ds(half * 256, 256)
        tp[:, cols] = (
            dot(jnp.where(first, h_t[...], zero), t_down[:N, cols])
            + dot(jnp.where(first, zero, h_t[...]), t_down[N:, cols])
        ).astype(BF)
    t_rs = to_y(lambda dy: tp.at[y_rows(dy)], lambda dy: rt.at[dy - 1])

    arrived(w_tok)
    arrived(d_rs)
    state[g_block()] = (s_tok[g_block()].astype(F32) + g_total(pd, rd)).astype(BF)
    d_ag = ag_g(state)
    k_ag = ag_z(coef)
    h_ag = ag_y(h_s)
    arrived(w_proj[2:])
    arrived(t_rs)
    arrived(d_ag)

    for half in range(2):
        cols = pl.ds(half * 256, 256)
        target = tp[y_rows(), cols].astype(F32)
        for index in range(3):
            target = target + rt[index, :, cols].astype(F32)
        pe[:, cols] = (dot(state[...], proj[:, cols]) - target).astype(BF)
    e_z = rs_z(pe, rez)
    s_aa = to_y(lambda dy: state.at[:, feat(dy)], lambda dy: state_f.at[y_rows()])
    state_f[y_rows(), :] = state[:, feat()]
    h_ag += relay_rows(h_ag, h_s)
    arrived(e_z)
    dp[s_rows(), :] = (
        (z_total(pe, rez) - t_in[s_rows(), :].astype(F32)) * (1.0 / math.sqrt(T))
    ).astype(BF)
    e_ag = ag_z(dp)
    arrived(k_ag)
    k_ay = ag_y(coef)
    arrived(e_ag)

    for tile in range(4):
        cols = pl.ds(tile * 256, 256)
        pf[:, cols] = dot_nt(dp[y_rows(), :], proj[cols, :]).astype(BF)
    f_rs = rs_g(pf, rf)
    p_ag = ag_y(dp)
    arrived(f_rs)
    d_state[g_block()] = g_total(pf, rf).astype(BF)
    f_ag = ag_g(d_state)
    p_ag += relay_rows(p_ag, dp)
    stores = []

    def store(src, dst):
        copy = pltpu.make_async_copy(src, dst, lsem.at[len(loads) + len(stores)])
        copy.start()
        stores.append(copy)

    store(xgt, xt_h)
    arrived(s_aa)
    state_t = state_f[...].T
    arrived(f_ag)

    d_hidden = dot_nt(d_state[:, :KS], down[0])
    for tile in range(1, 4):
        d_hidden += dot_nt(d_state[:, tile * KS : (tile + 1) * KS], down[tile])
    pg[...] = d_hidden.astype(BF)
    g_z = rs_z(pg, rgz)
    k_ay += relay_rows(k_ay, coef)
    d_aa = to_y(lambda dy: d_state.at[:, feat(dy)], lambda dy: d_state_f.at[y_rows()])
    d_state_f[y_rows(), :] = d_state[:, feat()]
    arrived(p_ag[2:])
    o_proj[...] = dot(state_t, dp[...]).astype(BF)
    store(o_proj, o_proj_h)
    arrived(g_z)
    dh[s_rows(), :] = z_total(pg, rgz).astype(BF)
    g_az = {dz: sems.start(dh.at[s_rows()], dh.at[s_rows()], s_dev(dz, 0)) for dz in (2, 1, 3)}
    g_ay = [sems.start(dh.at[s_rows()], dh.at[s_rows()], s_dev(0, dy)) for dy in (2, 1, 3)]
    arrived(h_ag[2:])
    arrived(d_aa)
    o_down[...] = dot(h_s[...].T, d_state_f[...]).astype(BF)
    store(o_down, o_down_h)
    for dz in (1, 3, 2):
        arrived([g_az[dz]])
        rows = s_rows(4 - dz)
        g_ay += [sems.start(dh.at[rows], dh.at[rows], s_dev(0, dy)) for dy in (2, 1, 3)]
    arrived(k_ay[2:])
    arrived(g_ay)
    for half in range(2):
        cols = pl.ds(half * N, N)
        dgu[:, cols] = (dh[...].astype(F32) * coef[:, cols].astype(F32)).astype(BF)
        store(dgu.at[:, cols], dgu_h.at[:, cols])

    for copy in sems.started:
        copy.wait_send()
    for copy in stores:
        copy.wait()


N_REMOTE = 160
N_LOCAL = 14 + 5


def results(
    xt_h, dgu_h, down_h, proj_h, o_gate_h, o_up_h, o_down_h, o_proj_h, xt, dgu, down, proj, out, sem
):
    gate, up = pl.ds(0, N), pl.ds(N, N)
    moves = [
        (xt_h, xt),
        (dgu_h.at[:, gate], dgu.at[:, gate]),
        (dgu_h.at[:, up], dgu.at[:, up]),
        (down_h, down),
        (proj_h, proj),
        (out.at[:, gate], o_gate_h),
        (out.at[:, up], o_up_h),
        (down, o_down_h),
        (proj, o_proj_h),
    ]
    copies = [
        pltpu.make_async_copy(src, dst, sem.at[index]) for index, (src, dst) in enumerate(moves)
    ]
    for copy in copies[:5]:
        copy.start()
    copies[0].wait()
    for half, cols in enumerate((gate, up)):
        copies[1 + half].wait()
        out[:, cols] = dot(xt[...], dgu[:, cols]).astype(BF)
        copies[5 + half].start()
        copies[3 + half].wait()
        copies[7 + half].start()
    for copy in copies[5:]:
        copy.wait()


def per_device(
    teacher_in, teacher_gain, teacher_gate, teacher_up, teacher_down, align_layer,
    student_in, student_gain, student_gate, student_up, student_down, projection,
):
    any_space = pl.BlockSpec(memory_space=pl.ANY)
    v = pltpu.VMEM
    scratch = [
        v((T, KT), BF), v((1, KT), F32), v((2 * KT, W2), BF), v((2 * N, KT), BF), v((1, T), jnp.int32),
        v((T, KS), BF), v((1, KS), F32), v((KS, W2), BF), v((4, N, KS), BF), v((4 * KS, KT), BF),
        v((64, 4 * KS), BF),
        v((T, KS), BF), v((KS, T), BF), v((T, 2 * KT), BF), v((T, 128), F32), v((T, N), BF),
        v((T, WS), BF), v((2, 32, WS), BF), v((2, 32, WS), BF), v((2, 64, WS), BF),
        v((3, 16, WS), BF), v((3, 16, WS), BF),
        v((T, N), BF), v((T, W2), BF),
        v((T, WS), BF), v((T // 2, WS), BF), v((T, WS), BF), v((7, 16, WS), BF),
        v((T, KT), BF), v((3, 64, KT), BF),
        v((64, 4 * KS), BF), v((15, 16, KS), BF), v((64, 4 * KS), BF),
        v((64, KT), BF), v((3, 16, KT), BF), v((T, KT), BF),
        v((64, 4 * KS), BF), v((15, 16, KS), BF), v((64, 4 * KS), BF),
        v((64, N), BF), v((3, 16, N), BF), v((T, N), BF), v((T, W2), BF),
        v((T, KS), BF), v((T, KS), BF),
        v((N, KS), BF), v((KS, KT), BF),
        pltpu.SemaphoreType.DMA((N_REMOTE,)),
        pltpu.SemaphoreType.DMA((N_REMOTE,)),
        pltpu.SemaphoreType.DMA((N_LOCAL,)),
    ]
    out = [
        jax.ShapeDtypeStruct((KS, T), BF),
        jax.ShapeDtypeStruct((T, W2), BF),
        jax.ShapeDtypeStruct((N, KS), BF),
        jax.ShapeDtypeStruct((KS, KT), BF),
    ]
    held = pl.pallas_call(
        kernel,
        name="distill",
        out_shape=out,
        in_specs=[any_space] * 12,
        out_specs=[any_space] * 4,
        scratch_shapes=scratch,
        cost_estimate=pl.CostEstimate(flops=3 * 10**9, bytes_accessed=10**7, transcendentals=10**5),
        compiler_params=pltpu.CompilerParams(
            collective_id=0, has_side_effects=True, vmem_limit_bytes=60 * 2**20
        ),
    )(
        teacher_in, teacher_gain.reshape(1, KT), teacher_gate, teacher_up,
        teacher_down.reshape(2 * N, KT), align_layer.reshape(1, T),
        student_in, student_gain.reshape(1, KS), student_gate, student_up, student_down, projection,
    )
    return pl.pallas_call(
        results,
        name="results",
        out_shape=[
            jax.ShapeDtypeStruct((KS, N), BF),
            jax.ShapeDtypeStruct((KS, N), BF),
            jax.ShapeDtypeStruct((N, KS), BF),
            jax.ShapeDtypeStruct((KS, KT), BF),
        ],
        in_specs=[any_space] * 4,
        out_specs=[any_space] * 4,
        scratch_shapes=[
            v((KS, T), BF), v((T, W2), BF), v((N, KS), BF), v((KS, KT), BF),
            v((KS, W2), BF), pltpu.SemaphoreType.DMA((9,)),
        ],
        cost_estimate=pl.CostEstimate(flops=3 * 10**8, bytes_accessed=4 * 10**6, transcendentals=0),
        compiler_params=pltpu.CompilerParams(vmem_limit_bytes=60 * 2**20),
    )(*held)


def solution(mesh):
    in_specs = (
        P(None, ("grp", "tp")),
        P(("grp", "tp")),
        P(None, ("grp", "tp"), "seq"),
        P(None, ("grp", "tp"), "seq"),
        P(None, "seq", ("grp", "tp")),
        P(),
        P(None, "seq"),
        P("seq"),
        P("seq", ("grp", "tp")),
        P("seq", ("grp", "tp")),
        P(("grp", "tp"), "seq"),
        P("seq", ("grp", "tp")),
    )
    out_specs = (
        P("seq", ("grp", "tp")),
        P("seq", ("grp", "tp")),
        P(("grp", "tp"), "seq"),
        P("seq", ("grp", "tp")),
    )
    return jax.shard_map(
        per_device, mesh=mesh, in_specs=in_specs, out_specs=out_specs, check_vma=False
    )
```
